256 devices in a mesh: seq: 8 (over y, x_hi), head: 32 (over z, x_lo, core).
Axes of the slice: x: 4 (x_hi: 2, x_lo: 2; x = x_hi * 2 + x_lo), y: 4, z: 8, core: 2. Of those that a mesh axis runs over, the one named last changes fastest.
Arguments:
- queries: bfloat16 [1024, 16384], P('seq', 'head'), may hold values from -15 to 15
- cache_keys: bfloat16 [8, 32, 1024, 128], P('seq', 'head'), may hold values from -4 to 4
- cache_values: bfloat16 [8, 32, 1024, 128], P('seq', 'head'), may hold values from -5 to 5
- new_keys: bfloat16 [1024, 1024], P('seq'), may hold values from -4 to 4
- new_values: bfloat16 [1024, 1024], P('seq'), may hold values from -5 to 5
- out_weight: bfloat16 [16384, 16384], P('head', 'seq'), may hold values from -0.0234375 to 0.0234375
- cache_lengths: int32 [8], replicated, may hold values from 1 to 4096, 16384 in all
- positions: int32 [1024], P('seq'), may hold values from 0 to 1023, each once
Outputs:
- mixed: bfloat16 [1024, 16384], P(('seq', 'head'))
The draws below stay inside these ranges and needn't reach their ends.
Inputs may be any that keep to these rules, and one draw needn't show every extreme that they name: `cache_lengths`: live slots of each group; they add up to 16384 and one group is full. `positions`: each of 0 to 1023 once.
All inputs are finite; a program needn't handle non-finite values.
Results may differ from the reference program's by a relative error of at most 0.0095.
Values may be sent and summed in bfloat16 or wider, within the bound.
No kernel may reach another device: no remote copies, remote signals or barrier semaphores. Data moves between devices by JAX's collectives and lax.ppermute only.
A program may use at most 128 MiB of HBM per device.

```python
import math
import jax
import jax.numpy as jnp
import numpy as np
from jax import lax

D = 16384
HQ = 128
KVH = 8
HD = 128
CACHE_DEV = 4096
QUAD = 4
CQ = 1024
NEW = 1024
N_SEQ = 8


def draw_queries(key, part):
    key = jax.random.fold_in(key, 11)
    drawn_values = 3.0 * jax.random.truncated_normal(key, -5.0, 5.0, (NEW, HQ * HD), jnp.float32)
    return drawn_values.astype(jnp.bfloat16)


def draw_cache_keys(key, part):
    key = jax.random.fold_in(key, 23)
    array_shape = (N_SEQ, KVH * QUAD, CQ, HD)
    drawn_values = jax.random.truncated_normal(key, -4.0, 4.0, array_shape, jnp.float32)
    return drawn_values.astype(jnp.bfloat16)


def levels(key, extent, pieces, smallest, largest):
    level = 1.0
    for position, blocks in pieces:
        steps = jax.random.uniform(jax.random.fold_in(jax.random.fold_in(key, 6), position), (blocks,), jnp.float32, smallest / len(pieces), largest / len(pieces))
        level = level * jnp.repeat(jnp.exp(steps), extent[position] // blocks).reshape((-1,) + (1,) * (len(extent) - 1 - position))
    return level


def length_profile(amount, total, limit, slope):
    portions = [(1 << 20) // math.isqrt(standing ** slope) + 1 for standing in range(2, amount + 1)]
    surplus, counts = total - limit - (amount - 1), [1] * (amount - 1)
    while surplus > 0:
        candidates = [i for i in range(amount - 1) if counts[i] < limit]
        mass, remaining = sum([portions[i] for i in candidates]), surplus
        for i in candidates:
            addition = min(limit - counts[i], max(1, remaining * portions[i] // mass), surplus)
            counts[i] = counts[i] + addition
            surplus = surplus - addition
    return np.array([limit] + counts)


def ragged_sizes(rng, amount, total, bound, skew):
    if amount == 2:
        one = jax.random.randint(rng, (), max(1, total - bound), min(bound, total - 1) + 1)
        return jnp.stack([one, total - one])
    tallies = jnp.asarray(length_profile(amount, total, bound, skew), jnp.int32)
    couples = (amount - 1) // 2
    giver, taker = tallies[1:1 + 2 * couples:2], tallies[2:2 + 2 * couples:2]
    margin = jnp.minimum(giver - 1, bound - taker)
    passed = jax.random.randint(jax.random.fold_in(rng, 1), (couples,), 0, 1 << 20) % (margin + 1)
    tallies = tallies.at[1:1 + 2 * couples:2].set(giver - passed).at[2:2 + 2 * couples:2].set(taker + passed)
    return tallies[jax.random.permutation(jax.random.fold_in(rng, 2), amount)]


def gaussian(stream_key, extent, scale, bound, split=(), held_as=jnp.bfloat16):
    drawn = scale * jax.random.normal(stream_key, extent, jnp.float32)
    if split:
        drawn = drawn * levels(stream_key, extent, split, -0.22, 0.18)
    return jnp.clip(drawn, -bound, bound).astype(held_as)


def setup_inputs(seed: int = 0) -> dict:
    key_of = jax.random.split(jax.random.key(seed), 9)
    queries = draw_queries(jax.random.fold_in(key_of[8], 71), 0)
    cache_keys = draw_cache_keys(jax.random.fold_in(key_of[8], 71), 0)
    cache_values = gaussian(key_of[2], (N_SEQ, KVH * QUAD, CQ, HD), 1.0, 5.0, ((0, 8), (1, 32)))
    new_keys = gaussian(key_of[3], (NEW, KVH * HD), 1.0, 4.0, ((0, 8),))
    new_values = gaussian(key_of[4], (NEW, KVH * HD), 1.0, 5.0, ((0, 8),))
    out_weight = gaussian(key_of[5], (HQ * HD, D), (4 * HQ * HD) ** -0.5, 0.0234375, ((0, 32), (1, 8)))
    cache_lengths = ragged_sizes(key_of[6], N_SEQ, N_SEQ * CACHE_DEV // 2, CACHE_DEV, 2).astype(jnp.int32)
    positions = jax.random.permutation(key_of[7], NEW).astype(jnp.int32)
    return dict(queries=queries, cache_keys=cache_keys, cache_values=cache_values, new_keys=new_keys, new_values=new_values, out_weight=out_weight, cache_lengths=cache_lengths, positions=positions)


def reference(queries, cache_keys, cache_values, new_keys, new_values, out_weight, cache_lengths, positions):
    group_size = HQ // KVH
    score_scale = 1.0 / math.sqrt(HD)
    key_table = cache_keys.reshape(N_SEQ, KVH, QUAD * CQ, HD)
    key_table = jnp.transpose(key_table, (1, 0, 2, 3)).reshape(KVH, N_SEQ * CACHE_DEV, HD)
    value_table = cache_values.reshape(N_SEQ, KVH, QUAD * CQ, HD)
    value_table = jnp.transpose(value_table, (1, 0, 2, 3)).reshape(KVH, N_SEQ * CACHE_DEV, HD)
    slot_index = jnp.arange(N_SEQ * CACHE_DEV, dtype=jnp.int32)
    live_slot = slot_index % CACHE_DEV < cache_lengths[slot_index // CACHE_DEV]
    new_key_heads = new_keys.reshape(NEW, KVH, HD)
    new_value_heads = new_values.reshape(NEW, KVH, HD)
    new_seen = positions[None, :] <= positions[:, None]

    def one_head(head_number):
        kv_head = head_number // group_size
        query_head = lax.dynamic_slice_in_dim(queries, head_number * HD, HD, 1)
        cache_rows = key_table[kv_head]
        cache_vals = value_table[kv_head]
        fresh_rows = new_key_heads[:, kv_head]
        fresh_vals = new_value_heads[:, kv_head]
        cache_scores = jnp.dot(query_head, cache_rows.T, preferred_element_type=jnp.float32) * score_scale
        fresh_scores = jnp.dot(query_head, fresh_rows.T, preferred_element_type=jnp.float32) * score_scale
        cache_scores = jnp.where(live_slot[None, :], cache_scores, -jnp.inf)
        fresh_scores = jnp.where(new_seen, fresh_scores, -jnp.inf)
        row_max = jnp.maximum(lax.optimization_barrier(jnp.max(cache_scores, axis=1)), lax.optimization_barrier(jnp.max(fresh_scores, axis=1)))
        cache_probs = jnp.exp(cache_scores - row_max[:, None])
        fresh_probs = jnp.exp(fresh_scores - row_max[:, None])
        denominator = lax.optimization_barrier(jnp.sum(cache_probs, axis=1)) + lax.optimization_barrier(jnp.sum(fresh_probs, axis=1))
        weighted = jnp.dot(cache_probs.astype(jnp.bfloat16), cache_vals, preferred_element_type=jnp.float32)
        weighted = weighted + jnp.dot(fresh_probs.astype(jnp.bfloat16), fresh_vals, preferred_element_type=jnp.float32)
        return (weighted / denominator[:, None]).astype(jnp.bfloat16)
    heads_out = lax.map(one_head, jnp.arange(HQ, dtype=jnp.int32))
    attended = jnp.transpose(heads_out, (1, 0, 2)).reshape(NEW, HQ * HD)
    return jnp.dot(attended, out_weight, preferred_element_type=jnp.float32).astype(jnp.bfloat16)
```

```python
import math

import jax
import jax.numpy as jnp
from jax import lax
from jax.experimental import pallas as pl
from jax.experimental.pallas import tpu as pltpu
from jax.sharding import Mesh, PartitionSpec as P

HD = 128
HEADS = 4
TOK = 128
SLOTS = 1024
ROWS = 2048
HEAD_ROWS = 512
BLOCK = 512
VROWS = HD + 16
NEG = -1e30
TO_LOG2 = math.log2(math.e) / math.sqrt(HD)
F32 = jnp.float32
BF16 = jnp.bfloat16
VMEM = pl.BlockSpec(memory_space=pltpu.VMEM)
SMEM = pl.BlockSpec(memory_space=pltpu.SMEM)


def moved(value, axis, size, step):
    return lax.ppermute(value, axis, [(i, (i + step) % size) for i in range(size)])


def along_y(value, step):
    return moved(value, "y", 4, step)


def along_x(value, step):
    return moved(value, ("xh", "xl"), 4, step)


def along_z(value, step):
    return moved(value, "z", 8, step)


def to_other_core(value):
    return moved(value, "core", 2, 1)


def params():
    return pltpu.CompilerParams(vmem_limit_bytes=48 * 2**20)


def absorb(keys2, values_t, visible, rows_t, m_ref, acc_ref):
    def score(head):
        cols = pl.ds(head * HEAD_ROWS, HEAD_ROWS)
        s = jnp.dot(keys2, rows_t[:, cols], preferred_element_type=F32)
        return jnp.where(visible, s, NEG)

    def update(head, s):
        cols = pl.ds(head * HEAD_ROWS, HEAD_ROWS)
        old = m_ref[:, cols]
        new = jnp.maximum(old, jnp.max(s, axis=0, keepdims=True))
        p = jnp.exp2(s - new).astype(BF16)
        m_ref[:, cols] = new
        acc_ref[:, cols] = acc_ref[:, cols] * jnp.exp2(old - new) + jnp.dot(
            values_t, p, preferred_element_type=F32
        )

    s = score(0)
    for head in range(HEADS):
        following = score(head + 1) if head + 1 < HEADS else None
        update(head, s)
        s = following


def with_ones(values):
    count = values.shape[0]
    return jnp.concatenate([values.T, jnp.ones((VROWS - HD, count), BF16)], axis=0)


def attend_body(first, last, chunks, *refs):
    refs = list(refs)
    live_ref = refs.pop(0)
    if first:
        q_refs = [refs.pop(0) for _ in range(4)]
        fresh_refs = [refs.pop(0) for _ in range(2)]
    else:
        rows_t, m_in, acc_in = refs.pop(0), refs.pop(0), refs.pop(0)
    k_refs = [refs.pop(0) for _ in range(chunks)]
    v_refs = [refs.pop(0) for _ in range(chunks)]
    if last:
        out_refs = [refs.pop(0) for _ in range(4)]
    else:
        if first:
            rows_t = refs.pop(0)
        m_out, acc_out = refs.pop(0), refs.pop(0)
    if last:
        m_ref, acc_ref = refs.pop(0), refs.pop(0)
    else:
        m_ref, acc_ref = m_out, acc_out
    keys2, values_t = refs

    if first:
        positions = []
        for i, q_ref in enumerate(q_refs):
            for head in range(HEADS):
                q = q_ref[0:TOK, head * HD : (head + 1) * HD].astype(F32).T * TO_LOG2
                high = q.astype(BF16)
                cols = slice(head * HEAD_ROWS + i * TOK, head * HEAD_ROWS + (i + 1) * TOK)
                rows_t[0:HD, cols] = high
                rows_t[HD : 2 * HD, cols] = (q - high.astype(F32)).astype(BF16)
            coded = q_ref[TOK : TOK + 16, 0:TOK].astype(F32)
            positions.append(coded[0:1] * 128.0 + coded[1:2])
        row_pos = jnp.concatenate(positions, axis=1)
        m_ref[...] = jnp.full(m_ref.shape, NEG, F32)
        acc_ref[...] = jnp.zeros(acc_ref.shape, F32)
    else:
        m_ref[...] = m_in[...]
        acc_ref[...] = acc_in[...]

    for j in range(chunks):
        k = k_refs[j][...]
        keys2[j, :, 0:HD] = k
        keys2[j, :, HD : 2 * HD] = k
        values_t[j] = with_ones(v_refs[j][...])

    @pl.loop(0, chunks)
    def _(j):
        live = live_ref[j]

        @pl.loop(0, (live + BLOCK - 1) // BLOCK)
        def _(b):
            offset = pl.multiple_of(b * BLOCK, BLOCK)
            slot = offset + lax.broadcasted_iota(jnp.int32, (BLOCK, HEAD_ROWS), 0)
            absorb(
                keys2[j, pl.ds(offset, BLOCK), :],
                values_t[j, :, pl.ds(offset, BLOCK)],
                slot < live,
                rows_t,
                m_ref,
                acc_ref,
            )

    if first:
        fresh_keys = jnp.concatenate([f[0:TOK] for f in fresh_refs], axis=0)
        fresh_values = jnp.concatenate([f[TOK : 2 * TOK] for f in fresh_refs], axis=0)
        coded = jnp.concatenate([f[2 * TOK : 3 * TOK] for f in fresh_refs], axis=0).astype(F32)
        key_pos = coded[:, 0:1] * 128.0 + coded[:, 1:2]
        absorb(
            jnp.concatenate([fresh_keys, fresh_keys], axis=1),
            with_ones(fresh_values),
            key_pos <= row_pos,
            rows_t,
            m_ref,
            acc_ref,
        )

    if last:
        for i, out_ref in enumerate(out_refs):
            for head in range(HEADS):
                start = head * HEAD_ROWS + i * TOK
                cols = slice(start, start + TOK)
                total = acc_ref[HD : HD + 1, cols]
                out_ref[head * HD : (head + 1) * HD, :] = (acc_ref[0:HD, cols] / total).astype(BF16)
            level = jnp.concatenate(
                [
                    m_ref[:, h * HEAD_ROWS + i * TOK : h * HEAD_ROWS + (i + 1) * TOK]
                    + jnp.log2(acc_ref[HD : HD + 1, h * HEAD_ROWS + i * TOK : h * HEAD_ROWS + (i + 1) * TOK])
                    for h in range(HEADS)
                ],
                axis=0,
            )
            high = level.astype(BF16).astype(F32)
            middle = (level - high).astype(BF16).astype(F32)
            low = level - high - middle
            stats = jnp.concatenate([high, middle, low, jnp.zeros((4, TOK), F32)], axis=0)
            out_ref[HEADS * HD : HEADS * HD + 16, :] = stats.astype(BF16)


def attend(first, last, live, state, keys, values):
    chunks = len(keys)
    operands = [live, *state, *keys, *values]
    running = [jax.ShapeDtypeStruct((1, ROWS), F32), jax.ShapeDtypeStruct((VROWS, ROWS), F32)]
    scratch = []
    if last:
        outs = [jax.ShapeDtypeStruct((HEADS * HD + 16, TOK), BF16)] * 4
        scratch = [pltpu.VMEM(r.shape, r.dtype) for r in running]
    elif first:
        outs = [jax.ShapeDtypeStruct((2 * HD, ROWS), BF16)] + running
    else:
        outs = running
    scratch += [
        pltpu.VMEM((chunks, SLOTS, 2 * HD), BF16),
        pltpu.VMEM((chunks, VROWS, SLOTS), BF16),
    ]
    return pl.pallas_call(
        lambda *refs: attend_body(first, last, chunks, *refs),
        out_shape=outs,
        in_specs=[SMEM] + [VMEM] * (len(operands) - 1),
        out_specs=[VMEM] * len(outs),
        scratch_shapes=scratch,
        compiler_params=params(),
        cost_estimate=pl.CostEstimate(
            flops=chunks * 3 * 10**9, bytes_accessed=4 * 2**20, transcendentals=0
        ),
        name="attend",
    )(*operands)


def merge_body(*refs):
    parts, out_ref = refs[:-1], refs[-1]
    levels = []
    for part in parts:
        coded = part[HEADS * HD : HEADS * HD + 16, :].astype(F32)
        levels.append(coded[0:4] + coded[4:8] + coded[8:12])
    top = levels[0]
    for level in levels[1:]:
        top = jnp.maximum(top, level)
    weights = [jnp.exp2(level - top) for level in levels]
    total = weights[0] + weights[1] + weights[2] + weights[3]
    weights = [w / total for w in weights]
    for head in range(HEADS):
        mixed = None
        for part, w in zip(parts, weights):
            term = part[head * HD : (head + 1) * HD, :].astype(F32) * w[head : head + 1]
            mixed = term if mixed is None else mixed + term
        out_ref[:, head * HD : (head + 1) * HD] = mixed.T.astype(BF16)


def merge(parts):
    return pl.pallas_call(
        merge_body,
        out_shape=jax.ShapeDtypeStruct((TOK, HEADS * HD), BF16),
        in_specs=[VMEM] * 4,
        out_specs=VMEM,
        compiler_params=params(),
        name="merge",
    )(*parts)


def project_body(z_ref, *refs):
    own, other = refs[0:4], refs[4:8]
    w_own, w_other = refs[8:10]
    outs = refs[10:19]
    x_ref = refs[19]
    width = own[0].shape[1]
    for r in range(8):
        part = pl.multiple_of(lax.rem(z_ref[0] + r, 8) * 16, 16)
        for j in range(4):
            row = r * 64 + j * 16
            x_ref[row : row + 16, 0:width] = own[j][pl.ds(part, 16), :]
            x_ref[row : row + 16, width : 2 * width] = other[j][pl.ds(part, 16), :]
    for n in range(4):
        cols = slice(n * 256, (n + 1) * 256)
        y = jnp.dot(x_ref[:, 0:width], w_own[:, cols], preferred_element_type=F32)
        y += jnp.dot(x_ref[:, width : 2 * width], w_other[:, cols], preferred_element_type=F32)
        y = y.astype(BF16)
        for r in range(8):
            if r < 4:
                outs[r][:, cols] = y[r * 64 : (r + 1) * 64]
            elif r == 4:
                outs[4][:, cols] = y[256:288]
                outs[5][:, cols] = y[288:320]
            else:
                outs[r + 1][:, cols] = y[r * 64 : (r + 1) * 64]


def project(z_index, own, other, w_own, w_other):
    full = jax.ShapeDtypeStruct((64, 1024), BF16)
    half = jax.ShapeDtypeStruct((32, 1024), BF16)
    return pl.pallas_call(
        project_body,
        out_shape=[full] * 4 + [half] * 2 + [full] * 3,
        in_specs=[SMEM] + [VMEM] * 10,
        out_specs=[VMEM] * 9,
        scratch_shapes=[pltpu.VMEM((512, 1024), BF16)],
        compiler_params=params(),
        cost_estimate=pl.CostEstimate(flops=10**9, bytes_accessed=4 * 2**20, transcendentals=0),
        name="project",
    )(z_index, *own, *other, w_own, w_other)


def sum_bf16(a, b):
    return (a.astype(F32) + b.astype(F32)).astype(BF16)


def sum_over_z(parts):
    up = along_z(parts[4], 1)
    down = along_z(parts[5], -1)
    p3 = parts[3]
    up = jnp.concatenate([sum_bf16(p3[:32], up), p3[32:]], axis=0)
    p5 = parts[6]
    down = jnp.concatenate([p5[:32], sum_bf16(p5[32:], down)], axis=0)
    for r in (2, 1):
        up = sum_bf16(parts[r], along_z(up, 1))
        down = sum_bf16(parts[9 - r], along_z(down, -1))
    return parts[0], along_z(up, 1), along_z(down, -1)


def order_body(place_ref, a0, a1, a2, b0, b1, b2, out_ref):
    for half, (p, u, d) in enumerate(((a0, a1, a2), (b0, b1, b2))):
        total = p[...].astype(F32) + u[...].astype(F32) + d[...].astype(F32)
        total = total.astype(BF16)
        for j in range(4):
            out_ref[place_ref[half * 4 + j]] = total[j * 16 : (j + 1) * 16]


def ordered(place, sums_a, sums_b):
    return pl.pallas_call(
        order_body,
        out_shape=jax.ShapeDtypeStruct((8, 16, 1024), BF16),
        in_specs=[SMEM] + [VMEM] * 6,
        out_specs=VMEM,
        compiler_params=params(),
        name="ordered",
    )(place, *sums_a, *sums_b)


def coded_positions(positions):
    return (positions // 128).astype(BF16), (positions % 128).astype(BF16)


def shards(
    queries, cache_keys, cache_values, new_keys, new_values, out_weight, cache_lengths, positions
):
    y, xh, z = lax.axis_index("y"), lax.axis_index("xh"), lax.axis_index("z")
    xl, core = lax.axis_index("xl"), lax.axis_index("core")
    x = xh * 2 + xl
    keys, values = cache_keys[0, 0], cache_values[0, 0]

    def live_of(step, other):
        place = (x + step) % 4
        group = y * 2 + place // 2
        quarter = (place % 2) * 2 + (core + other) % 2
        return jnp.clip(cache_lengths[group] - quarter * SLOTS, 0, SLOTS)

    def lives(*steps):
        return jnp.stack([live_of(s, o) for s in steps for o in (0, 1)])

    high, low = coded_positions(positions)
    q_ext = jnp.concatenate(
        [queries, jnp.pad(jnp.stack([high, low]), ((0, 14), (0, 512 - TOK)))], axis=0
    )
    fresh = jnp.concatenate(
        [
            lax.dynamic_slice_in_dim(new_keys, z * HD, HD, 1),
            lax.dynamic_slice_in_dim(new_values, z * HD, HD, 1),
            jnp.pad(jnp.stack([high, low], axis=1), ((0, 0), (0, HD - 2))),
        ],
        axis=0,
    )
    fresh_far = along_x(fresh, 2)
    left_k, right_v = along_x(keys, 1), along_x(values, -1)
    q_prev, q_next, q_far = along_y(q_ext, 1), along_y(q_ext, -1), along_y(q_ext, 2)
    other_k, other_v = to_other_core(keys), to_other_core(values)
    left_v, right_k = along_x(values, 1), along_x(keys, -1)
    far_k, far_v = along_x(left_k, 1), along_x(right_v, -1)

    state = attend(
        True,
        False,
        lives(0),
        (q_ext, q_prev, q_next, q_far, fresh, fresh_far),
        (keys, other_k),
        (values, other_v),
    )
    rows_t, m, acc = state
    m, acc = attend(
        False,
        False,
        lives(-1, 1),
        (rows_t, m, acc),
        (left_k, to_other_core(left_k), right_k, to_other_core(right_k)),
        (left_v, to_other_core(left_v), right_v, to_other_core(right_v)),
    )
    mine, prev, following, far = attend(
        False,
        True,
        lives(2),
        (rows_t, m, acc),
        (far_k, to_other_core(far_k)),
        (far_v, to_other_core(far_v)),
    )
    attended = merge((mine, along_y(prev, -1), along_y(following, 1), along_y(far, 2)))

    w_own = lax.dynamic_slice_in_dim(out_weight, core * 1024, 1024, 1)
    w_other = to_other_core(lax.dynamic_slice_in_dim(out_weight, (1 - core) * 1024, 1024, 1))

    z_index = z[None]

    def gathered(block):
        blocks = (block, along_y(block, 1), along_y(block, -1), along_y(block, 2))
        return blocks, tuple(to_other_core(b) for b in blocks)

    across = along_x(attended, 2)
    sums_a = sum_over_z(project(z_index, *gathered(attended), w_own, w_other))
    sums_b = sum_over_z(project(z_index, *gathered(across), w_own, w_other))

    ys = jnp.stack([y, y + 3, y + 1, y + 2]) % 4
    place = jnp.concatenate([ys * 2 + xh, ys * 2 + 1 - xh]).astype(jnp.int32)
    blocks = ordered(place, sums_a, sums_b).reshape(128, 1024)
    spread = lax.all_to_all(blocks, ("y", "xh", "xl", "core"), 0, 0, tiled=True)
    spread = spread.reshape(8, 2, 2, 4, 1024).astype(F32)
    total = (spread[:, 0] + spread[:, 1]).astype(BF16)
    return jnp.transpose(total, (2, 0, 1, 3)).reshape(4, 16384)


def solution(mesh):
    fine = Mesh(mesh.devices.reshape(4, 2, 8, 2, 2), ("y", "xh", "z", "xl", "core"))
    seq, head = ("y", "xh"), ("z", "xl", "core")
    placed = (
        P(seq, head),
        P(seq, head, None, None),
        P(seq, head, None, None),
        P(seq, None),
        P(seq, None),
        P(head, seq),
        P(),
        P(seq),
    )
    return jax.shard_map(
        shards, mesh=fine, in_specs=placed, out_specs=P(seq + head, None), check_vma=False
    )
```

```python
import math

import jax
import jax.numpy as jnp
from jax import lax
from jax.experimental import pallas as pl
from jax.experimental.pallas import tpu as pltpu
from jax.sharding import Mesh, PartitionSpec as P

HD = 128
HEADS = 4
TOK = 128
SLOTS = 1024
ROWS = 2048
HEAD_ROWS = 512
BLOCK = 1024
VROWS = HD + 16
NEG = -1e30
FRESH = 32
WIDE = 1024
TO_LOG2 = math.log2(math.e) / math.sqrt(HD)
F32 = jnp.float32
BF16 = jnp.bfloat16
VMEM = pl.BlockSpec(memory_space=pltpu.VMEM)
SMEM = pl.BlockSpec(memory_space=pltpu.SMEM)
HBM = pl.BlockSpec(memory_space=pltpu.HBM)


def moved(value, axis, size, step):
    return lax.ppermute(value, axis, [(i, (i + step) % size) for i in range(size)])


def along_y(value, step):
    return moved(value, ("yp", "yl"), 4, step)


def to_y_pair(value, flip):
    pairs = []
    for y in range(4):
        for core in range(2):
            other = y ^ 1 if core == flip else (y + (1 if y % 2 else 3)) % 4
            pairs.append((y * 2 + core, other * 2 + core))
    return lax.ppermute(value, ("yp", "yl", "core"), pairs)


def y_index():
    return lax.axis_index("yp") * 2 + lax.axis_index("yl")


def along_x(value, step):
    return moved(value, ("xh", "xl"), 4, step)


def along_z(value, step):
    return moved(value, "z", 8, step)


def to_other_core(value):
    return moved(value, "core", 2, 1)


def after(value, earlier):
    return lax.optimization_barrier((value, earlier))[0]


def params(mib):
    return pltpu.CompilerParams(vmem_limit_bytes=mib * 2**20)


def pack_body(q_hbm, k_hbm, v_hbm, nk_hbm, nv_hbm, pos_ref, q_out, kv_out, col_ref, sems):
    z = lax.axis_index("z")
    quarter = lax.axis_index("xl") * 2 + lax.axis_index("core")
    lanes = pl.ds(pl.multiple_of(z * HD, HD), HD)
    rows = pl.ds(pl.multiple_of(quarter * FRESH, FRESH), FRESH)
    start = 2 * SLOTS
    copies = [
        pltpu.make_async_copy(source, target, sems.at[i])
        for i, (source, target) in enumerate(
            (
                (q_hbm, q_out.at[pl.ds(0, TOK)]),
                (k_hbm, kv_out.at[pl.ds(0, SLOTS)]),
                (v_hbm, kv_out.at[pl.ds(SLOTS, SLOTS)]),
                (nk_hbm.at[rows, lanes], kv_out.at[pl.ds(start, FRESH)]),
                (nv_hbm.at[rows, lanes], kv_out.at[pl.ds(start + FRESH, FRESH)]),
            )
        )
    ]
    for copy in copies:
        copy.start()
    pos = jnp.broadcast_to(pos_ref[...].astype(F32), (TOK, TOK))
    high = jnp.floor(pos * (1.0 / 128.0))
    low = pos - high * 128.0
    q_out[TOK : TOK + 16, :] = jnp.zeros((16, HEADS * HD), BF16)
    row = lax.broadcasted_iota(jnp.int32, (16, TOK), 0)
    coded = jnp.where(row == 0, high[0:16], jnp.where(row == 1, low[0:16], 0.0))
    q_out[TOK : TOK + 16, 0:TOK] = coded.astype(BF16)
    col_ref[...] = high.T
    kv_out[start + 2 * FRESH : start + 3 * FRESH, :] = col_ref[rows, :].astype(BF16)
    col_ref[...] = low.T
    kv_out[start + 3 * FRESH : start + 4 * FRESH, :] = col_ref[rows, :].astype(BF16)
    for copy in copies:
        copy.wait()


def pack(queries, keys, values, new_keys, new_values, positions):
    return pl.pallas_call(
        pack_body,
        out_shape=[
            jax.ShapeDtypeStruct((TOK + 16, HEADS * HD), BF16),
            jax.ShapeDtypeStruct((2 * SLOTS + 4 * FRESH, HD), BF16),
        ],
        in_specs=[HBM] * 5 + [VMEM],
        out_specs=[VMEM] * 2,
        scratch_shapes=[pltpu.VMEM((TOK, TOK), F32), pltpu.SemaphoreType.DMA((5,))],
        name="pack",
    )(queries, keys, values, new_keys, new_values, positions)


def halves_body(w_hbm, w_kept, w_away, sems):
    core = lax.axis_index("core")
    copies = [
        pltpu.make_async_copy(
            w_hbm.at[:, pl.ds(pl.multiple_of(half * WIDE, WIDE), WIDE)], target, sems.at[i]
        )
        for i, (half, target) in enumerate(((core, w_kept), (1 - core, w_away)))
    ]
    for copy in copies:
        copy.start()
    for copy in copies:
        copy.wait()


def halves(weight):
    return pl.pallas_call(
        halves_body,
        out_shape=[jax.ShapeDtypeStruct((weight.shape[0], WIDE), BF16)] * 2,
        in_specs=[HBM],
        out_specs=[VMEM] * 2,
        scratch_shapes=[pltpu.SemaphoreType.DMA((2,))],
        name="halves",
    )(weight)


def update(s, values_t, cols, m_ref, acc_ref):
    old = m_ref[:, cols]
    new = jnp.maximum(old, jnp.max(s, axis=0, keepdims=True))
    p = jnp.exp2(s - new).astype(BF16)
    m_ref[:, cols] = new
    acc_ref[:, cols] = acc_ref[:, cols] * jnp.exp2(old - new) + jnp.dot(
        values_t, p, preferred_element_type=F32
    )


def flash(block_count, base_ref, keys2, values_t, rows_t, m_ref, acc_ref, s_ref):
    def place(step):
        cols = pl.multiple_of((step % HEADS) * HEAD_ROWS, HEAD_ROWS)
        base = pl.multiple_of(base_ref[step // HEADS], BLOCK)
        return pl.ds(base, BLOCK), pl.ds(cols, HEAD_ROWS)

    def score(step, slot):
        at, cols = place(step)
        s_ref[slot] = jnp.dot(keys2[at, :], rows_t[:, cols], preferred_element_type=F32)

    def settle(step, slot):
        at, cols = place(step)
        update(s_ref[slot], values_t[:, at], cols, m_ref, acc_ref)

    steps = block_count * HEADS

    @pl.when(steps > 0)
    def _():
        score(0, 0)

    @pl.loop(0, steps // 2)
    def _(i):
        score(2 * i + 1, 1)
        settle(2 * i, 0)
        score(jnp.minimum(2 * i + 2, steps - 1), 0)
        settle(2 * i + 1, 1)


def absorb_fresh(carry_ref, kv_refs, rows_t, row_pos, m_ref, acc_ref):
    def fresh(part):
        pieces = []
        for j in range(carry_ref.shape[0] // (4 * FRESH)):
            start = (j * 4 + part) * FRESH
            pieces.append(carry_ref[start : start + FRESH, :])
        for kv in kv_refs:
            start = 2 * SLOTS + part * FRESH
            pieces.append(kv[start : start + FRESH, :])
        return jnp.concatenate(pieces, axis=0)

    keys = fresh(0)
    keys = jnp.concatenate([keys, keys], axis=1)
    values = fresh(1).astype(F32).T
    ones = jnp.ones((VROWS - HD, values.shape[1]), F32)
    values_t = jnp.concatenate([values, ones], axis=0).astype(BF16)
    key_pos = fresh(2).astype(F32) * 128.0 + fresh(3).astype(F32)
    seen = jnp.concatenate([key_pos] * (HEAD_ROWS // TOK), axis=1) <= row_pos[...]

    def score(head):
        cols = slice(head * HEAD_ROWS, (head + 1) * HEAD_ROWS)
        s = jnp.dot(keys, rows_t[:, cols], preferred_element_type=F32)
        return jnp.where(seen, s, NEG)

    s = score(0)
    for head in range(HEADS):
        following = score(head + 1) if head + 1 < HEADS else None
        cols = slice(head * HEAD_ROWS, (head + 1) * HEAD_ROWS)
        update(s, values_t, cols, m_ref, acc_ref)
        s = following


def attend_body(first, last, sources, *refs):
    refs = list(refs)
    chunks = len(sources)
    len_ref = refs.pop(0)
    if first:
        q_refs = [refs.pop(0) for _ in range(4)]
    else:
        rows_t, row_pos, m_in, acc_in, carry_in = [refs.pop(0) for _ in range(5)]
    kv_refs = [refs.pop(0) for _ in range(chunks)]
    if last:
        out_refs = [refs.pop(0) for _ in range(4)]
    else:
        if first:
            rows_t, row_pos = refs.pop(0), refs.pop(0)
        m_out, acc_out, carry_out = [refs.pop(0) for _ in range(3)]
    if last:
        m_ref, acc_ref = refs.pop(0), refs.pop(0)
    else:
        m_ref, acc_ref = m_out, acc_out
    keys2, values_t, base_ref, s_ref = refs

    if first:
        for i, q_ref in enumerate(q_refs):
            for head in range(HEADS):
                q = q_ref[0:TOK, head * HD : (head + 1) * HD].astype(F32).T * TO_LOG2
                high = q.astype(BF16)
                cols = slice(head * HEAD_ROWS + i * TOK, head * HEAD_ROWS + (i + 1) * TOK)
                rows_t[0:HD, cols] = high
                rows_t[HD : 2 * HD, cols] = (q - high.astype(F32)).astype(BF16)
            coded = q_ref[TOK : TOK + 16, 0:TOK].astype(F32)
            row_pos[:, i * TOK : (i + 1) * TOK] = coded[0:1] * 128.0 + coded[1:2]
        m_ref[...] = jnp.full(m_ref.shape, NEG, F32)
        acc_ref[...] = jnp.zeros(acc_ref.shape, F32)
    else:
        m_ref[...] = m_in[...]
        acc_ref[...] = acc_in[...]

    x = lax.axis_index("xh") * 2 + lax.axis_index("xl")
    block_count = jnp.int32(0)
    for j, (step, swapped) in enumerate(sources):
        there = lax.rem(x + step, 4)
        group = y_index() * 2 + there // 2
        quarter = lax.rem(there, 2) * 2 + lax.rem(lax.axis_index("core") + swapped, 2)
        live = jnp.clip(len_ref[group] - quarter * SLOTS, 0, SLOTS)
        at = slice(j * SLOTS, (j + 1) * SLOTS)
        alive = lax.broadcasted_iota(jnp.int32, (SLOTS, HD), 0) < live
        k = kv_refs[j][0:SLOTS, :].astype(F32)
        k = jnp.where(alive, k, k[0:1, :]).astype(BF16)
        keys2[at, 0:HD] = k
        keys2[at, HD : 2 * HD] = k
        alive = lax.broadcasted_iota(jnp.int32, (VROWS, SLOTS), 1) < live
        v = jnp.concatenate(
            [kv_refs[j][SLOTS : 2 * SLOTS, :].astype(F32).T, jnp.ones((VROWS - HD, SLOTS), F32)],
            axis=0,
        )
        values_t[:, at] = jnp.where(alive, v, 0.0).astype(BF16)
        for b in range(SLOTS // BLOCK):
            base_ref[block_count] = j * SLOTS + b * BLOCK
            block_count += (live > b * BLOCK).astype(jnp.int32)

    if not last:
        held = 0 if first else carry_in.shape[0]
        if held:
            carry_out[0:held, :] = carry_in[...]
        for j, kv in enumerate(kv_refs):
            at = held + j * 4 * FRESH
            carry_out[at : at + 4 * FRESH, :] = kv[2 * SLOTS : 2 * SLOTS + 4 * FRESH, :]
    else:
        absorb_fresh(carry_in, kv_refs, rows_t, row_pos, m_ref, acc_ref)

    flash(block_count, base_ref, keys2, values_t, rows_t, m_ref, acc_ref, s_ref)

    if last:
        for i, out_ref in enumerate(out_refs):
            levels = []
            for head in range(HEADS):
                start = head * HEAD_ROWS + i * TOK
                cols = slice(start, start + TOK)
                total = acc_ref[HD : HD + 1, cols]
                out_ref[head * HD : (head + 1) * HD, :] = (acc_ref[0:HD, cols] / total).astype(BF16)
                levels.append(m_ref[:, cols] + jnp.log2(total))
            level = jnp.concatenate(levels, axis=0)
            high = level.astype(BF16).astype(F32)
            middle = (level - high).astype(BF16).astype(F32)
            low = level - high - middle
            stats = jnp.concatenate([high, middle, low, jnp.zeros((4, TOK), F32)], axis=0)
            out_ref[HEADS * HD : HEADS * HD + 16, :] = stats.astype(BF16)


def attend(first, last, lengths, state, sources, bundles):
    operands = [lengths, *state, *bundles]
    running = [jax.ShapeDtypeStruct((1, ROWS), F32), jax.ShapeDtypeStruct((VROWS, ROWS), F32)]
    scratch = []
    if last:
        outs = [jax.ShapeDtypeStruct((HEADS * HD + 16, TOK), BF16)] * 4
        scratch = [pltpu.VMEM(r.shape, r.dtype) for r in running]
    elif first:
        outs = [
            jax.ShapeDtypeStruct((2 * HD, ROWS), BF16),
            jax.ShapeDtypeStruct((1, HEAD_ROWS), F32),
        ] + running
    else:
        outs = running
    if not last:
        held = 0 if first else state[-1].shape[0]
        outs = outs + [jax.ShapeDtypeStruct((held + len(sources) * 4 * FRESH, HD), BF16)]
    slots = len(sources) * SLOTS
    scratch += [
        pltpu.VMEM((slots, 2 * HD), BF16),
        pltpu.VMEM((VROWS, slots), BF16),
        pltpu.SMEM((slots // BLOCK + 1,), jnp.int32),
        pltpu.VMEM((2, BLOCK, HEAD_ROWS), F32),
    ]
    return pl.pallas_call(
        lambda *refs: attend_body(first, last, sources, *refs),
        out_shape=outs,
        in_specs=[SMEM] + [VMEM] * (len(operands) - 1),
        out_specs=[VMEM] * len(outs),
        scratch_shapes=scratch,
        compiler_params=params(26),
        cost_estimate=pl.CostEstimate(
            flops=10**6, bytes_accessed=2**10, transcendentals=0
        ),
        name="attend",
    )(*operands)


def merge_body(*refs):
    parts, out_ref = refs[:-1], refs[-1]
    levels = []
    for part in parts:
        coded = part[HEADS * HD : HEADS * HD + 16, :].astype(F32)
        levels.append(coded[0:4] + coded[4:8] + coded[8:12])
    top = levels[0]
    for level in levels[1:]:
        top = jnp.maximum(top, level)
    weights = [jnp.exp2(level - top) for level in levels]
    total = weights[0] + weights[1] + weights[2] + weights[3]
    weights = [w / total for w in weights]
    for head in range(HEADS):
        mixed = None
        for part, w in zip(parts, weights):
            term = part[head * HD : (head + 1) * HD, :].astype(F32) * w[head : head + 1]
            mixed = term if mixed is None else mixed + term
        out_ref[:, head * HD : (head + 1) * HD] = mixed.T.astype(BF16)


def merge(parts):
    return pl.pallas_call(
        merge_body,
        out_shape=jax.ShapeDtypeStruct((TOK, HEADS * HD), BF16),
        in_specs=[VMEM] * 4,
        out_specs=VMEM,
        compiler_params=params(4),
        name="merge",
    )(*parts)


def project_body(*refs):
    x_own, x_other = refs[0:2]
    weights = refs[2:6]
    outs = refs[6:24]
    x_ref, w_ref, sems = refs[24:27]
    depth = weights[0].shape[0]
    copies = [
        pltpu.make_async_copy(
            weight, w_ref.at[i // 2, pl.ds((i % 2) * depth, depth)], sems.at[i]
        )
        for i, weight in enumerate(weights)
    ]
    for copy in copies:
        copy.start()
    z = lax.axis_index("z")
    for r in range(8):
        part = pl.multiple_of(lax.rem(z + r, 8) * 16, 16)
        for j in range(4):
            row = r * 64 + j * 16
            source = pl.ds(pl.multiple_of(part + j * TOK, 16), 16)
            x_ref[row : row + 16, 0:depth] = x_own[source, :]
            x_ref[row : row + 16, depth : 2 * depth] = x_other[source, :]
    for copy in copies:
        copy.wait()
    for side in range(2):
        out = outs[side * 9 : side * 9 + 9]
        for n in range(4):
            cols = slice(n * 256, (n + 1) * 256)
            y = jnp.dot(x_ref[...], w_ref[side, :, cols], preferred_element_type=F32).astype(BF16)
            for r in range(8):
                if r < 4:
                    out[r][:, cols] = y[r * 64 : (r + 1) * 64]
                elif r == 4:
                    out[4][:, cols] = y[256:288]
                    out[5][:, cols] = y[288:320]
                else:
                    out[r + 1][:, cols] = y[r * 64 : (r + 1) * 64]


def project(x_own, x_other, weights):
    full = jax.ShapeDtypeStruct((64, WIDE), BF16)
    half = jax.ShapeDtypeStruct((32, WIDE), BF16)
    outs = pl.pallas_call(
        project_body,
        out_shape=([full] * 4 + [half] * 2 + [full] * 3) * 2,
        in_specs=[VMEM] * 2 + [HBM] * 4,
        out_specs=[VMEM] * 18,
        scratch_shapes=[
            pltpu.VMEM((512, 1024), BF16),
            pltpu.VMEM((2, 1024, WIDE), BF16),
            pltpu.SemaphoreType.DMA((4,)),
        ],
        compiler_params=params(16),
        name="project",
    )(x_own, x_other, *weights)
    return outs[:9], outs[9:]


def sum_bf16(a, b):
    return (a.astype(F32) + b.astype(F32)).astype(BF16)


def sum_over_z(parts):
    up = along_z(parts[4], 1)
    down = along_z(parts[5], -1)
    p3 = parts[3]
    half = p3.shape[0] // 2
    up = jnp.concatenate([sum_bf16(p3[:half], up), p3[half:]], axis=0)
    p5 = parts[6]
    down = jnp.concatenate([p5[:half], sum_bf16(p5[half:], down)], axis=0)
    for r in (2, 1):
        up = sum_bf16(parts[r], along_z(up, 1))
        down = sum_bf16(parts[9 - r], along_z(down, -1))
    return parts[0], along_z(up, 1), along_z(down, -1)


def order_body(*refs):
    out_ref = refs[6]
    yp, yl, xh = (lax.axis_index(name) for name in ("yp", "yl", "xh"))
    for side in range(2):
        kept, up, down = refs[side * 3 : side * 3 + 3]
        total = kept[...].astype(F32) + up[...].astype(F32) + down[...].astype(F32)
        total = total.astype(BF16)
        column = pl.ds(pl.multiple_of((yl if side == 0 else 1 - yl) * WIDE, WIDE), WIDE)
        for j in range(4):
            place = (yp if j % 2 == 0 else 1 - yp) * 2 + (xh if j < 2 else 1 - xh)
            out_ref[place, :, column] = total[j * 16 : (j + 1) * 16]


def ordered(sums):
    return pl.pallas_call(
        order_body,
        out_shape=jax.ShapeDtypeStruct((4, 16, 2 * WIDE), BF16),
        in_specs=[VMEM] * 6,
        out_specs=VMEM,
        compiler_params=params(4),
        name="ordered",
    )(*sums)


def shards(
    queries, cache_keys, cache_values, new_keys, new_values, out_weight, cache_lengths, positions
):
    q_ext, kv = pack(
        queries, cache_keys[0, 0], cache_values[0, 0], new_keys, new_values, positions[None, :]
    )
    left, right = along_x(kv, 1), along_x(kv, -1)
    q_prev, q_next, q_far = along_y(q_ext, 1), along_y(q_ext, -1), along_y(q_ext, 2)
    q_all = (q_prev, q_next, q_far)
    far = along_x(after(kv, q_all), 2)
    w_kept, w_away = halves(after(out_weight, q_all))
    w_kept_pair, w_away_pair = to_y_pair(w_kept, 0), to_y_pair(w_away, 1)
    left, right = after((left, right), w_kept)
    rows_t, row_pos, m, acc, carry = attend(
        True,
        False,
        cache_lengths,
        (q_ext, *q_all),
        ((0, 0), (3, 0), (1, 0)),
        (kv, left, right),
    )
    left_other, right_other = to_other_core(left), to_other_core(right)
    other = to_other_core(after(kv, m))
    m, acc, carry = attend(
        False,
        False,
        cache_lengths,
        (rows_t, row_pos, m, acc, carry),
        ((3, 1), (1, 1), (0, 1)),
        (left_other, right_other, other),
    )
    far_other = to_other_core(far)
    mine, prev, following, distant = attend(
        False,
        True,
        cache_lengths,
        (rows_t, row_pos, m, acc, carry),
        ((2, 0), (2, 1)),
        (far, far_other),
    )
    attended = merge((mine, along_y(prev, -1), along_y(following, 1), along_y(distant, 2)))

    attended, w_kept_pair, w_away_pair = lax.optimization_barrier(
        (attended, w_kept_pair, w_away_pair)
    )
    w_other, w_other_pair = to_other_core(w_away), to_other_core(w_away_pair)

    x_own = jnp.concatenate(
        [
            attended,
            along_y(attended, 2),
            along_x(attended, 2),
            lax.ppermute(attended, ("yp", "xh"), [(i, 3 - i) for i in range(4)]),
        ],
        axis=0,
    )
    weights = (w_kept, w_other, w_kept_pair, w_other_pair)
    near, pair = project(x_own, to_other_core(x_own), weights)
    blocks = ordered((*sum_over_z(near), *sum_over_z(pair))).reshape(64, 2 * WIDE)
    spread = lax.all_to_all(blocks, ("yp", "xh", "xl", "core"), 0, 0, tiled=True)
    spread = spread.reshape(2, 2, 2, 2, 4, 2, WIDE).astype(F32)
    total = (spread[:, :, 0] + spread[:, :, 1]).astype(BF16)
    own = (jnp.arange(2) == lax.axis_index("yl"))[:, None]
    second = jnp.where(own, total[:, :, 1], total[::-1, :, 1])
    total = jnp.stack([total[:, :, 0], second], axis=2)
    return jnp.transpose(total, (3, 0, 4, 1, 2, 5)).reshape(4, 16384)


def solution(mesh):
    fine = Mesh(
        mesh.devices.reshape(2, 2, 2, 8, 2, 2), ("yp", "yl", "xh", "z", "xl", "core")
    )
    seq, head = ("yp", "yl", "xh"), ("z", "xl", "core")
    placed = (
        P(seq, head),
        P(seq, head, None, None),
        P(seq, head, None, None),
        P(seq, None),
        P(seq, None),
        P(head, seq),
        P(),
        P(seq),
    )
    return jax.shard_map(
        shards, mesh=fine, in_specs=placed, out_specs=P(seq + head, None), check_vma=False
    )
```

```python
import math

import jax
import jax.numpy as jnp
from jax import lax
from jax.experimental import pallas as pl
from jax.experimental.pallas import tpu as pltpu
from jax.sharding import Mesh, PartitionSpec as P

HD = 128
HEADS = 4
TOK = 128
SLOTS = 1024
ROWS = 2048
HEAD_ROWS = 512
BLOCK = 1024
VROWS = HD + 16
NEG = -1e30
FRESH = 32
WIDE = 1024
TO_LOG2 = math.log2(math.e) / math.sqrt(HD)
F32 = jnp.float32
BF16 = jnp.bfloat16
VMEM = pl.BlockSpec(memory_space=pltpu.VMEM)
SMEM = pl.BlockSpec(memory_space=pltpu.SMEM)
HBM = pl.BlockSpec(memory_space=pltpu.HBM)


def moved(value, axis, size, step):
    return lax.ppermute(value, axis, [(i, (i + step) % size) for i in range(size)])


def along_y(value, step):
    return moved(value, ("yp", "yl"), 4, step)


def to_y_pair(value, flip):
    pairs = []
    for y in range(4):
        for core in range(2):
            other = y ^ 1 if core == flip else (y + (1 if y % 2 else 3)) % 4
            pairs.append((y * 2 + core, other * 2 + core))
    return lax.ppermute(value, ("yp", "yl", "core"), pairs)


def y_index():
    return lax.axis_index("yp") * 2 + lax.axis_index("yl")


def along_x(value, step):
    return moved(value, ("xh", "xl"), 4, step)


def along_z(value, step):
    return moved(value, "z", 8, step)


def to_other_core(value):
    return moved(value, "core", 2, 1)


def after(value, earlier):
    return lax.optimization_barrier((value, earlier))[0]


def params(mib):
    return pltpu.CompilerParams(vmem_limit_bytes=mib * 2**20)


def pack_body(q_hbm, k_hbm, v_hbm, nk_hbm, nv_hbm, pos_ref, q_out, kv_out, col_ref, sems):
    z = lax.axis_index("z")
    quarter = lax.axis_index("xl") * 2 + lax.axis_index("core")
    lanes = pl.ds(pl.multiple_of(z * HD, HD), HD)
    rows = pl.ds(pl.multiple_of(quarter * FRESH, FRESH), FRESH)
    start = 2 * SLOTS
    copies = [
        pltpu.make_async_copy(source, target, sems.at[i])
        for i, (source, target) in enumerate(
            (
                (q_hbm, q_out.at[pl.ds(0, TOK)]),
                (k_hbm, kv_out.at[pl.ds(0, SLOTS)]),
                (v_hbm, kv_out.at[pl.ds(SLOTS, SLOTS)]),
                (nk_hbm.at[rows, lanes], kv_out.at[pl.ds(start, FRESH)]),
                (nv_hbm.at[rows, lanes], kv_out.at[pl.ds(start + FRESH, FRESH)]),
            )
        )
    ]
    for copy in copies:
        copy.start()
    pos = jnp.broadcast_to(pos_ref[...].astype(F32), (TOK, TOK))
    high = jnp.floor(pos * (1.0 / 128.0))
    low = pos - high * 128.0
    q_out[TOK : TOK + 16, :] = jnp.zeros((16, HEADS * HD), BF16)
    row = lax.broadcasted_iota(jnp.int32, (16, TOK), 0)
    coded = jnp.where(row == 0, high[0:16], jnp.where(row == 1, low[0:16], 0.0))
    q_out[TOK : TOK + 16, 0:TOK] = coded.astype(BF16)
    col_ref[...] = high.T
    kv_out[start + 2 * FRESH : start + 3 * FRESH, :] = col_ref[rows, :].astype(BF16)
    col_ref[...] = low.T
    kv_out[start + 3 * FRESH : start + 4 * FRESH, :] = col_ref[rows, :].astype(BF16)
    for copy in copies:
        copy.wait()


def pack(queries, keys, values, new_keys, new_values, positions):
    return pl.pallas_call(
        pack_body,
        out_shape=[
            jax.ShapeDtypeStruct((TOK + 16, HEADS * HD), BF16),
            jax.ShapeDtypeStruct((2 * SLOTS + 4 * FRESH, HD), BF16),
        ],
        in_specs=[HBM] * 5 + [VMEM],
        out_specs=[VMEM] * 2,
        scratch_shapes=[pltpu.VMEM((TOK, TOK), F32), pltpu.SemaphoreType.DMA((5,))],
        name="pack",
    )(queries, keys, values, new_keys, new_values, positions)


def halves_body(w_hbm, w_kept, w_away, sems):
    core = lax.axis_index("core")
    copies = [
        pltpu.make_async_copy(
            w_hbm.at[:, pl.ds(pl.multiple_of(half * WIDE, WIDE), WIDE)], target, sems.at[i]
        )
        for i, (half, target) in enumerate(((core, w_kept), (1 - core, w_away)))
    ]
    for copy in copies:
        copy.start()
    for copy in copies:
        copy.wait()


def halves(weight):
    return pl.pallas_call(
        halves_body,
        out_shape=[jax.ShapeDtypeStruct((weight.shape[0], WIDE), BF16)] * 2,
        in_specs=[HBM],
        out_specs=[VMEM] * 2,
        scratch_shapes=[pltpu.SemaphoreType.DMA((2,))],
        name="halves",
    )(weight)


def update(s, values_t, cols, m_ref, acc_ref):
    old = m_ref[:, cols]
    new = jnp.maximum(old, jnp.max(s, axis=0, keepdims=True))
    p = jnp.exp2(s - new).astype(BF16)
    m_ref[:, cols] = new
    acc_ref[:, cols] = acc_ref[:, cols] * jnp.exp2(old - new) + jnp.dot(
        values_t, p, preferred_element_type=F32
    )


def flash(block_count, base_ref, keys2, values_t, rows_t, m_ref, acc_ref, s_ref):
    def place(step):
        cols = pl.multiple_of((step % HEADS) * HEAD_ROWS, HEAD_ROWS)
        base = pl.multiple_of(base_ref[step // HEADS], BLOCK)
        return pl.ds(base, BLOCK), pl.ds(cols, HEAD_ROWS)

    def score(step, slot):
        at, cols = place(step)
        s_ref[slot] = jnp.dot(keys2[at, :], rows_t[:, cols], preferred_element_type=F32)

    def settle(step, slot):
        at, cols = place(step)
        update(s_ref[slot], values_t[:, at], cols, m_ref, acc_ref)

    steps = block_count * HEADS

    @pl.when(steps > 0)
    def _():
        score(0, 0)

    @pl.loop(0, steps // 2)
    def _(i):
        score(2 * i + 1, 1)
        settle(2 * i, 0)
        score(jnp.minimum(2 * i + 2, steps - 1), 0)
        settle(2 * i + 1, 1)


def absorb_fresh(carry_ref, kv_refs, rows_t, row_pos, m_ref, acc_ref):
    def fresh(part):
        pieces = []
        for j in range(carry_ref.shape[0] // (4 * FRESH)):
            start = (j * 4 + part) * FRESH
            pieces.append(carry_ref[start : start + FRESH, :])
        for kv in kv_refs:
            start = 2 * SLOTS + part * FRESH
            pieces.append(kv[start : start + FRESH, :])
        return jnp.concatenate(pieces, axis=0)

    keys = fresh(0)
    keys = jnp.concatenate([keys, keys], axis=1)
    values = fresh(1).astype(F32).T
    ones = jnp.ones((VROWS - HD, values.shape[1]), F32)
    values_t = jnp.concatenate([values, ones], axis=0).astype(BF16)
    key_pos = fresh(2).astype(F32) * 128.0 + fresh(3).astype(F32)
    seen = jnp.concatenate([key_pos] * (HEAD_ROWS // TOK), axis=1) <= row_pos[...]

    def score(head):
        cols = slice(head * HEAD_ROWS, (head + 1) * HEAD_ROWS)
        s = jnp.dot(keys, rows_t[:, cols], preferred_element_type=F32)
        return jnp.where(seen, s, NEG)

    s = score(0)
    for head in range(HEADS):
        following = score(head + 1) if head + 1 < HEADS else None
        cols = slice(head * HEAD_ROWS, (head + 1) * HEAD_ROWS)
        update(s, values_t, cols, m_ref, acc_ref)
        s = following


def attend_body(first, last, sources, *refs):
    refs = list(refs)
    chunks = len(sources)
    len_ref = refs.pop(0)
    if first:
        q_refs = [refs.pop(0) for _ in range(4)]
    else:
        rows_t, row_pos, m_in, acc_in, carry_in = [refs.pop(0) for _ in range(5)]
    kv_refs = [refs.pop(0) for _ in range(chunks)]
    if last:
        out_refs = [refs.pop(0) for _ in range(4)]
    else:
        if first:
            rows_t, row_pos = refs.pop(0), refs.pop(0)
        m_out, acc_out, carry_out = [refs.pop(0) for _ in range(3)]
    if last:
        m_ref, acc_ref = refs.pop(0), refs.pop(0)
    else:
        m_ref, acc_ref = m_out, acc_out
    keys2, values_t, base_ref, s_ref = refs

    if first:
        for i, q_ref in enumerate(q_refs):
            for head in range(HEADS):
                q = q_ref[0:TOK, head * HD : (head + 1) * HD].astype(F32).T * TO_LOG2
                high = q.astype(BF16)
                cols = slice(head * HEAD_ROWS + i * TOK, head * HEAD_ROWS + (i + 1) * TOK)
                rows_t[0:HD, cols] = high
                rows_t[HD : 2 * HD, cols] = (q - high.astype(F32)).astype(BF16)
            coded = q_ref[TOK : TOK + 16, 0:TOK].astype(F32)
            row_pos[:, i * TOK : (i + 1) * TOK] = coded[0:1] * 128.0 + coded[1:2]
        m_ref[...] = jnp.full(m_ref.shape, NEG, F32)
        acc_ref[...] = jnp.zeros(acc_ref.shape, F32)
    else:
        m_ref[...] = m_in[...]
        acc_ref[...] = acc_in[...]

    x = lax.axis_index("xh") * 2 + lax.axis_index("xl")
    block_count = jnp.int32(0)
    for j, (step, swapped) in enumerate(sources):
        there = lax.rem(x + step, 4)
        group = y_index() * 2 + there // 2
        quarter = lax.rem(there, 2) * 2 + lax.rem(lax.axis_index("core") + swapped, 2)
        live = jnp.clip(len_ref[group] - quarter * SLOTS, 0, SLOTS)
        at = slice(j * SLOTS, (j + 1) * SLOTS)
        alive = lax.broadcasted_iota(jnp.int32, (SLOTS, HD), 0) < live
        k = kv_refs[j][0:SLOTS, :].astype(F32)
        k = jnp.where(alive, k, k[0:1, :]).astype(BF16)
        keys2[at, 0:HD] = k
        keys2[at, HD : 2 * HD] = k
        alive = lax.broadcasted_iota(jnp.int32, (VROWS, SLOTS), 1) < live
        v = jnp.concatenate(
            [kv_refs[j][SLOTS : 2 * SLOTS, :].astype(F32).T, jnp.ones((VROWS - HD, SLOTS), F32)],
            axis=0,
        )
        values_t[:, at] = jnp.where(alive, v, 0.0).astype(BF16)
        for b in range(SLOTS // BLOCK):
            base_ref[block_count] = j * SLOTS + b * BLOCK
            block_count += (live > b * BLOCK).astype(jnp.int32)

    if not last:
        held = 0 if first else carry_in.shape[0]
        if held:
            carry_out[0:held, :] = carry_in[...]
        for j, kv in enumerate(kv_refs):
            at = held + j * 4 * FRESH
            carry_out[at : at + 4 * FRESH, :] = kv[2 * SLOTS : 2 * SLOTS + 4 * FRESH, :]
    else:
        absorb_fresh(carry_in, kv_refs, rows_t, row_pos, m_ref, acc_ref)

    flash(block_count, base_ref, keys2, values_t, rows_t, m_ref, acc_ref, s_ref)

    if last:
        for i, out_ref in enumerate(out_refs):
            levels = []
            for head in range(HEADS):
                start = head * HEAD_ROWS + i * TOK
                cols = slice(start, start + TOK)
                total = acc_ref[HD : HD + 1, cols]
                out_ref[head * HD : (head + 1) * HD, :] = (acc_ref[0:HD, cols] / total).astype(BF16)
                levels.append(m_ref[:, cols] + jnp.log2(total))
            level = jnp.concatenate(levels, axis=0)
            high = level.astype(BF16).astype(F32)
            middle = (level - high).astype(BF16).astype(F32)
            low = level - high - middle
            stats = jnp.concatenate([high, middle, low, jnp.zeros((4, TOK), F32)], axis=0)
            out_ref[HEADS * HD : HEADS * HD + 16, :] = stats.astype(BF16)


def attend(first, last, lengths, state, sources, bundles):
    operands = [lengths, *state, *bundles]
    running = [jax.ShapeDtypeStruct((1, ROWS), F32), jax.ShapeDtypeStruct((VROWS, ROWS), F32)]
    scratch = []
    if last:
        outs = [jax.ShapeDtypeStruct((HEADS * HD + 16, TOK), BF16)] * 4
        scratch = [pltpu.VMEM(r.shape, r.dtype) for r in running]
    elif first:
        outs = [
            jax.ShapeDtypeStruct((2 * HD, ROWS), BF16),
            jax.ShapeDtypeStruct((1, HEAD_ROWS), F32),
        ] + running
    else:
        outs = running
    if not last:
        held = 0 if first else state[-1].shape[0]
        outs = outs + [jax.ShapeDtypeStruct((held + len(sources) * 4 * FRESH, HD), BF16)]
    slots = len(sources) * SLOTS
    scratch += [
        pltpu.VMEM((slots, 2 * HD), BF16),
        pltpu.VMEM((VROWS, slots), BF16),
        pltpu.SMEM((slots // BLOCK + 1,), jnp.int32),
        pltpu.VMEM((2, BLOCK, HEAD_ROWS), F32),
    ]
    return pl.pallas_call(
        lambda *refs: attend_body(first, last, sources, *refs),
        out_shape=outs,
        in_specs=[SMEM] + [VMEM] * (len(operands) - 1),
        out_specs=[VMEM] * len(outs),
        scratch_shapes=scratch,
        compiler_params=params(26),
        cost_estimate=pl.CostEstimate(
            flops=10**6, bytes_accessed=2**10, transcendentals=0
        ),
        name="attend",
    )(*operands)


def merge_body(*refs):
    parts, out_ref = refs[:-1], refs[-1]
    levels = []
    for part in parts:
        coded = part[HEADS * HD : HEADS * HD + 16, :].astype(F32)
        levels.append(coded[0:4] + coded[4:8] + coded[8:12])
    top = levels[0]
    for level in levels[1:]:
        top = jnp.maximum(top, level)
    weights = [jnp.exp2(level - top) for level in levels]
    total = weights[0] + weights[1] + weights[2] + weights[3]
    weights = [w / total for w in weights]
    for head in range(HEADS):
        mixed = None
        for part, w in zip(parts, weights):
            term = part[head * HD : (head + 1) * HD, :].astype(F32) * w[head : head + 1]
            mixed = term if mixed is None else mixed + term
        out_ref[:, head * HD : (head + 1) * HD] = mixed.T.astype(BF16)


def merge(parts):
    return pl.pallas_call(
        merge_body,
        out_shape=jax.ShapeDtypeStruct((TOK, HEADS * HD), BF16),
        in_specs=[VMEM] * 4,
        out_specs=VMEM,
        compiler_params=params(4),
        name="merge",
    )(*parts)


def project_body(*refs):
    x_own, x_other = refs[0:2]
    weights = refs[2:6]
    outs = refs[6:24]
    x_ref, w_ref, sems = refs[24:27]
    depth = weights[0].shape[0]
    copies = [
        pltpu.make_async_copy(
            weight, w_ref.at[i // 2, pl.ds((i % 2) * depth, depth)], sems.at[i]
        )
        for i, weight in enumerate(weights)
    ]
    for copy in copies:
        copy.start()
    z = lax.axis_index("z")
    for r in range(8):
        part = pl.multiple_of(lax.rem(z + r, 8) * 16, 16)
        for j in range(4):
            row = r * 64 + j * 16
            source = pl.ds(pl.multiple_of(part + j * TOK, 16), 16)
            x_ref[row : row + 16, 0:depth] = x_own[source, :]
            x_ref[row : row + 16, depth : 2 * depth] = x_other[source, :]
    for copy in copies:
        copy.wait()
    for side in range(2):
        out = outs[side * 9 : side * 9 + 9]
        for n in range(4):
            cols = slice(n * 256, (n + 1) * 256)
            y = jnp.dot(x_ref[...], w_ref[side, :, cols], preferred_element_type=F32).astype(BF16)
            for r in range(8):
                if r < 4:
                    out[r][:, cols] = y[r * 64 : (r + 1) * 64]
                elif r == 4:
                    out[4][:, cols] = y[256:288]
                    out[5][:, cols] = y[288:320]
                else:
                    out[r + 1][:, cols] = y[r * 64 : (r + 1) * 64]


def project(x_own, x_other, weights):
    full = jax.ShapeDtypeStruct((64, WIDE), BF16)
    half = jax.ShapeDtypeStruct((32, WIDE), BF16)
    outs = pl.pallas_call(
        project_body,
        out_shape=([full] * 4 + [half] * 2 + [full] * 3) * 2,
        in_specs=[VMEM] * 2 + [HBM] * 4,
        out_specs=[VMEM] * 18,
        scratch_shapes=[
            pltpu.VMEM((512, 1024), BF16),
            pltpu.VMEM((2, 1024, WIDE), BF16),
            pltpu.SemaphoreType.DMA((4,)),
        ],
        compiler_params=params(16),
        name="project",
    )(x_own, x_other, *weights)
    return outs[:9], outs[9:]


def sum_bf16(a, b):
    return (a.astype(F32) + b.astype(F32)).astype(BF16)


def sum_over_z(parts):
    up = along_z(parts[4], 1)
    down = along_z(parts[5], -1)
    p3 = parts[3]
    half = p3.shape[0] // 2
    up = jnp.concatenate([sum_bf16(p3[:half], up), p3[half:]], axis=0)
    p5 = parts[6]
    down = jnp.concatenate([p5[:half], sum_bf16(p5[half:], down)], axis=0)
    for r in (2, 1):
        up = sum_bf16(parts[r], along_z(up, 1))
        down = sum_bf16(parts[9 - r], along_z(down, -1))
    return parts[0], along_z(up, 1), along_z(down, -1)


def order_body(*refs):
    out_ref = refs[6]
    yp, yl, xh = (lax.axis_index(name) for name in ("yp", "yl", "xh"))
    for side in range(2):
        kept, up, down = refs[side * 3 : side * 3 + 3]
        total = kept[...].astype(F32) + up[...].astype(F32) + down[...].astype(F32)
        total = total.astype(BF16)
        column = pl.ds(pl.multiple_of((yl if side == 0 else 1 - yl) * WIDE, WIDE), WIDE)
        for j in range(4):
            place = (yp if j % 2 == 0 else 1 - yp) * 2 + (xh if j < 2 else 1 - xh)
            out_ref[place, :, column] = total[j * 16 : (j + 1) * 16]


def ordered(sums):
    return pl.pallas_call(
        order_body,
        out_shape=jax.ShapeDtypeStruct((4, 16, 2 * WIDE), BF16),
        in_specs=[VMEM] * 6,
        out_specs=VMEM,
        compiler_params=params(4),
        name="ordered",
    )(*sums)


def finish_body(spread_ref, out_ref, sum_ref):
    yl = lax.axis_index("yl")
    for side in range(2):
        cols = slice(side * WIDE, (side + 1) * WIDE)
        for p in range(2):
            for xh in range(2):
                for core in range(2):
                    first = (p * 2 + xh) * 16 + core * 4
                    sum_ref[p, xh, core] = (
                        spread_ref[first : first + 4, cols].astype(F32)
                        + spread_ref[first + 8 : first + 12, cols].astype(F32)
                    )
        own = yl == side
        for p in range(2):
            for xh in range(2):
                for core in range(2):
                    value = sum_ref[p, xh, core]
                    if core == 1:
                        value = jnp.where(own, value, sum_ref[1 - p, xh, core])
                    start = (((p * 2 + side) * 2 + xh) * 2 + core) * WIDE
                    out_ref[:, start : start + WIDE] = value.astype(BF16)


def finish(spread):
    return pl.pallas_call(
        finish_body,
        out_shape=jax.ShapeDtypeStruct((4, 16 * WIDE), BF16),
        in_specs=[VMEM],
        out_specs=VMEM,
        scratch_shapes=[pltpu.VMEM((2, 2, 2, 4, WIDE), F32)],
        compiler_params=params(4),
        name="finish",
    )(spread)


def shards(
    queries, cache_keys, cache_values, new_keys, new_values, out_weight, cache_lengths, positions
):
    q_ext, kv = pack(
        queries, cache_keys[0, 0], cache_values[0, 0], new_keys, new_values, positions[None, :]
    )
    left, right = along_x(kv, 1), along_x(kv, -1)
    q_prev, q_next, q_far = along_y(q_ext, 1), along_y(q_ext, -1), along_y(q_ext, 2)
    q_all = (q_prev, q_next, q_far)
    w_kept, w_away = halves(after(out_weight, q_prev))
    other = to_other_core(after(kv, q_all))
    w_kept_pair, w_away_pair = to_y_pair(w_kept, 0), to_y_pair(w_away, 1)
    left, right = after((left, right), w_kept)
    far = along_x(after(kv, (left, right)), 2)
    rows_t, row_pos, m, acc, carry = attend(
        True,
        False,
        cache_lengths,
        (q_ext, *q_all),
        ((0, 0), (0, 1), (3, 0), (1, 0)),
        (kv, other, left, right),
    )
    left_other, right_other = to_other_core(left), to_other_core(right)
    far_other = to_other_core(after(far, m))
    mine, prev, following, distant = attend(
        False,
        True,
        cache_lengths,
        (rows_t, row_pos, m, acc, carry),
        ((3, 1), (1, 1), (2, 0), (2, 1)),
        (left_other, right_other, far, far_other),
    )
    attended = merge((mine, along_y(prev, -1), along_y(following, 1), along_y(distant, 2)))

    attended, w_kept_pair, w_away_pair = lax.optimization_barrier(
        (attended, w_kept_pair, w_away_pair)
    )
    w_other, w_other_pair = to_other_core(w_away), to_other_core(w_away_pair)

    corner = lax.ppermute(attended, ("yp", "xh"), [(i, 3 - i) for i in range(4)])
    blocks = (attended, along_y(attended, 2), along_x(attended, 2), corner)
    x_own = jnp.concatenate(blocks, axis=0)
    weights = (w_kept, w_other, w_kept_pair, w_other_pair)
    near, pair = project(x_own, to_other_core(x_own), weights)
    blocks = ordered((*sum_over_z(near), *sum_over_z(pair))).reshape(64, 2 * WIDE)
    spread = lax.all_to_all(blocks, ("yp", "xh", "xl", "core"), 0, 0, tiled=True)
    return finish(spread)


def solution(mesh):
    fine = Mesh(
        mesh.devices.reshape(2, 2, 2, 8, 2, 2), ("yp", "yl", "xh", "z", "xl", "core")
    )
    seq, head = ("yp", "yl", "xh"), ("z", "xl", "core")
    placed = (
        P(seq, head),
        P(seq, head, None, None),
        P(seq, head, None, None),
        P(seq, None),
        P(seq, None),
        P(head, seq),
        P(),
        P(seq),
    )
    return jax.shard_map(
        shards, mesh=fine, in_specs=placed, out_specs=P(seq + head, None), check_vma=False
    )
```

```python
import math

import jax
import jax.numpy as jnp
from jax import lax
from jax.experimental import pallas as pl
from jax.experimental.pallas import tpu as pltpu
from jax.sharding import Mesh, PartitionSpec as P

HD = 128
HEADS = 4
TOK = 128
SLOTS = 1024
ROWS = 2048
HEAD_ROWS = 512
BLOCK = 1024
VROWS = HD + 16
NEG = -1e30
FRESH = 32
WIDE = 1024
TO_LOG2 = math.log2(math.e) / math.sqrt(HD)
F32 = jnp.float32
BF16 = jnp.bfloat16
VMEM = pl.BlockSpec(memory_space=pltpu.VMEM)
SMEM = pl.BlockSpec(memory_space=pltpu.SMEM)
HBM = pl.BlockSpec(memory_space=pltpu.HBM)


def moved(value, axis, size, step):
    return lax.ppermute(value, axis, [(i, (i + step) % size) for i in range(size)])


def along_y(value, step):
    return moved(value, ("yp", "yl"), 4, step)


def to_y_pair(value, swap):
    pairs = []
    for y in range(4):
        for core in range(2):
            there = 1 - core if swap else core
            other = y ^ 1 if there == 0 else (y + (1 if y % 2 else 3)) % 4
            pairs.append((y * 2 + core, other * 2 + there))
    return lax.ppermute(value, ("yp", "yl", "core"), pairs)


def y_index():
    return lax.axis_index("yp") * 2 + lax.axis_index("yl")


def along_x(value, step):
    return moved(value, ("xh", "xl"), 4, step)


def along_z(value, step):
    return moved(value, "z", 8, step)


def to_other_core(value):
    return moved(value, "core", 2, 1)


def after(value, earlier):
    return lax.optimization_barrier((value, earlier))[0]


def params(mib):
    return pltpu.CompilerParams(vmem_limit_bytes=mib * 2**20)


def pack_body(q_hbm, k_hbm, v_hbm, nk_hbm, nv_hbm, pos_ref, q_out, kv_out, col_ref, sems):
    z = lax.axis_index("z")
    quarter = lax.axis_index("xl") * 2 + lax.axis_index("core")
    lanes = pl.ds(pl.multiple_of(z * HD, HD), HD)
    rows = pl.ds(pl.multiple_of(quarter * FRESH, FRESH), FRESH)
    start = 2 * SLOTS
    copies = [
        pltpu.make_async_copy(source, target, sems.at[i])
        for i, (source, target) in enumerate(
            (
                (q_hbm, q_out.at[pl.ds(0, TOK)]),
                (k_hbm, kv_out.at[pl.ds(0, SLOTS)]),
                (v_hbm, kv_out.at[pl.ds(SLOTS, SLOTS)]),
                (nk_hbm.at[rows, lanes], kv_out.at[pl.ds(start, FRESH)]),
                (nv_hbm.at[rows, lanes], kv_out.at[pl.ds(start + FRESH, FRESH)]),
            )
        )
    ]
    for copy in copies:
        copy.start()
    pos = jnp.broadcast_to(pos_ref[...].astype(F32), (TOK, TOK))
    high = jnp.floor(pos * (1.0 / 128.0))
    low = pos - high * 128.0
    q_out[TOK : TOK + 16, :] = jnp.zeros((16, HEADS * HD), BF16)
    row = lax.broadcasted_iota(jnp.int32, (16, TOK), 0)
    coded = jnp.where(row == 0, high[0:16], jnp.where(row == 1, low[0:16], 0.0))
    q_out[TOK : TOK + 16, 0:TOK] = coded.astype(BF16)
    col_ref[...] = high.T
    kv_out[start + 2 * FRESH : start + 3 * FRESH, :] = col_ref[rows, :].astype(BF16)
    col_ref[...] = low.T
    kv_out[start + 3 * FRESH : start + 4 * FRESH, :] = col_ref[rows, :].astype(BF16)
    for copy in copies:
        copy.wait()


def pack(queries, keys, values, new_keys, new_values, positions):
    return pl.pallas_call(
        pack_body,
        out_shape=[
            jax.ShapeDtypeStruct((TOK + 16, HEADS * HD), BF16),
            jax.ShapeDtypeStruct((2 * SLOTS + 4 * FRESH, HD), BF16),
        ],
        in_specs=[HBM] * 5 + [VMEM],
        out_specs=[VMEM] * 2,
        scratch_shapes=[pltpu.VMEM((TOK, TOK), F32), pltpu.SemaphoreType.DMA((5,))],
        name="pack",
    )(queries, keys, values, new_keys, new_values, positions)


def halves_body(w_hbm, w_kept, w_away, sems):
    core = lax.axis_index("core")
    copies = [
        pltpu.make_async_copy(
            w_hbm.at[:, pl.ds(pl.multiple_of(half * WIDE, WIDE), WIDE)], target, sems.at[i]
        )
        for i, (half, target) in enumerate(((core, w_kept), (1 - core, w_away)))
    ]
    for copy in copies:
        copy.start()
    for copy in copies:
        copy.wait()


def halves(weight):
    return pl.pallas_call(
        halves_body,
        out_shape=[jax.ShapeDtypeStruct((weight.shape[0], WIDE), BF16)] * 2,
        in_specs=[HBM],
        out_specs=[VMEM] * 2,
        scratch_shapes=[pltpu.SemaphoreType.DMA((2,))],
        name="halves",
    )(weight)


def update(s, top, values_t, cols, m_ref, acc_ref):
    old = m_ref[:, cols]
    new = jnp.maximum(old, top)
    p = jnp.exp2(s - new).astype(BF16)
    m_ref[:, cols] = new
    acc_ref[:, cols] = acc_ref[:, cols] * jnp.exp2(old - new) + jnp.dot(
        values_t, p, preferred_element_type=F32
    )


def flash(block_count, base_ref, keys2, values_t, rows_t, m_ref, acc_ref, s_ref, top_ref):
    def place(step):
        cols = pl.multiple_of((step % HEADS) * HEAD_ROWS, HEAD_ROWS)
        base = pl.multiple_of(base_ref[step // HEADS], BLOCK)
        return pl.ds(base, BLOCK), pl.ds(cols, HEAD_ROWS)

    def score(step, slot):
        at, cols = place(step)
        s = jnp.dot(keys2[at, :], rows_t[:, cols], preferred_element_type=F32)
        s_ref[slot] = s
        top_ref[slot] = jnp.max(s, axis=0, keepdims=True)

    def settle(step, slot):
        at, cols = place(step)
        update(s_ref[slot], top_ref[slot], values_t[:, at], cols, m_ref, acc_ref)

    steps = block_count * HEADS

    @pl.when(steps > 0)
    def _():
        score(0, 0)

    @pl.loop(0, steps // 2)
    def _(i):
        score(2 * i + 1, 1)
        settle(2 * i, 0)
        score(jnp.minimum(2 * i + 2, steps - 1), 0)
        settle(2 * i + 1, 1)


def absorb_fresh(carry_ref, kv_refs, rows_t, row_pos, m_ref, acc_ref):
    def fresh(part):
        pieces = []
        for j in range(carry_ref.shape[0] // (4 * FRESH)):
            start = (j * 4 + part) * FRESH
            pieces.append(carry_ref[start : start + FRESH, :])
        for kv in kv_refs:
            start = 2 * SLOTS + part * FRESH
            pieces.append(kv[start : start + FRESH, :])
        return jnp.concatenate(pieces, axis=0)

    keys = fresh(0)
    keys = jnp.concatenate([keys, keys], axis=1)
    values = fresh(1).astype(F32).T
    ones = jnp.ones((VROWS - HD, values.shape[1]), F32)
    values_t = jnp.concatenate([values, ones], axis=0).astype(BF16)
    key_pos = fresh(2).astype(F32) * 128.0 + fresh(3).astype(F32)
    seen = jnp.concatenate([key_pos] * (HEAD_ROWS // TOK), axis=1) <= row_pos[...]

    def score(head):
        cols = slice(head * HEAD_ROWS, (head + 1) * HEAD_ROWS)
        s = jnp.dot(keys, rows_t[:, cols], preferred_element_type=F32)
        return jnp.where(seen, s, NEG)

    s = score(0)
    for head in range(HEADS):
        following = score(head + 1) if head + 1 < HEADS else None
        cols = slice(head * HEAD_ROWS, (head + 1) * HEAD_ROWS)
        top = jnp.max(s, axis=0, keepdims=True)
        update(s, top, values_t, cols, m_ref, acc_ref)
        s = following


def attend_body(first, last, sources, *refs):
    refs = list(refs)
    chunks = len(sources)
    len_ref = refs.pop(0)
    if first:
        q_refs = [refs.pop(0) for _ in range(4)]
    else:
        rows_t, row_pos, m_in, acc_in, carry_in = [refs.pop(0) for _ in range(5)]
    kv_refs = [refs.pop(0) for _ in range(chunks)]
    if last:
        out_refs = [refs.pop(0) for _ in range(4)]
    else:
        if first:
            rows_t, row_pos = refs.pop(0), refs.pop(0)
        m_out, acc_out, carry_out = [refs.pop(0) for _ in range(3)]
    if last:
        m_ref, acc_ref = refs.pop(0), refs.pop(0)
    else:
        m_ref, acc_ref = m_out, acc_out
    keys2, values_t, base_ref, s_ref, top_ref = refs

    if first:
        for i, q_ref in enumerate(q_refs):
            for head in range(HEADS):
                q = q_ref[0:TOK, head * HD : (head + 1) * HD].astype(F32).T * TO_LOG2
                high = q.astype(BF16)
                cols = slice(head * HEAD_ROWS + i * TOK, head * HEAD_ROWS + (i + 1) * TOK)
                rows_t[0:HD, cols] = high
                rows_t[HD : 2 * HD, cols] = (q - high.astype(F32)).astype(BF16)
            coded = q_ref[TOK : TOK + 16, 0:TOK].astype(F32)
            row_pos[:, i * TOK : (i + 1) * TOK] = coded[0:1] * 128.0 + coded[1:2]
        m_ref[...] = jnp.full(m_ref.shape, NEG, F32)
        acc_ref[...] = jnp.zeros(acc_ref.shape, F32)
    else:
        m_ref[...] = m_in[...]
        acc_ref[...] = acc_in[...]

    x = lax.axis_index("xh") * 2 + lax.axis_index("xl")
    block_count = jnp.int32(0)
    for j, (step, swapped) in enumerate(sources):
        there = lax.rem(x + step, 4)
        group = y_index() * 2 + there // 2
        quarter = lax.rem(there, 2) * 2 + lax.rem(lax.axis_index("core") + swapped, 2)
        live = jnp.clip(len_ref[group] - quarter * SLOTS, 0, SLOTS)
        at = slice(j * SLOTS, (j + 1) * SLOTS)
        alive = lax.broadcasted_iota(jnp.int32, (SLOTS, HD), 0) < live
        k = kv_refs[j][0:SLOTS, :].astype(F32)
        k = jnp.where(alive, k, k[0:1, :]).astype(BF16)
        keys2[at, 0:HD] = k
        keys2[at, HD : 2 * HD] = k
        alive = lax.broadcasted_iota(jnp.int32, (VROWS, SLOTS), 1) < live
        v = jnp.concatenate(
            [kv_refs[j][SLOTS : 2 * SLOTS, :].astype(F32).T, jnp.ones((VROWS - HD, SLOTS), F32)],
            axis=0,
        )
        values_t[:, at] = jnp.where(alive, v, 0.0).astype(BF16)
        for b in range(SLOTS // BLOCK):
            base_ref[block_count] = j * SLOTS + b * BLOCK
            block_count += (live > b * BLOCK).astype(jnp.int32)

    if not last:
        held = 0 if first else carry_in.shape[0]
        if held:
            carry_out[0:held, :] = carry_in[...]
        for j, kv in enumerate(kv_refs):
            at = held + j * 4 * FRESH
            carry_out[at : at + 4 * FRESH, :] = kv[2 * SLOTS : 2 * SLOTS + 4 * FRESH, :]
    else:
        absorb_fresh(carry_in, kv_refs, rows_t, row_pos, m_ref, acc_ref)

    flash(block_count, base_ref, keys2, values_t, rows_t, m_ref, acc_ref, s_ref, top_ref)

    if last:
        for i, out_ref in enumerate(out_refs):
            levels = []
            for head in range(HEADS):
                start = head * HEAD_ROWS + i * TOK
                cols = slice(start, start + TOK)
                total = acc_ref[HD : HD + 1, cols]
                out_ref[head * HD : (head + 1) * HD, :] = (acc_ref[0:HD, cols] / total).astype(BF16)
                levels.append(m_ref[:, cols] + jnp.log2(total))
            level = jnp.concatenate(levels, axis=0)
            high = level.astype(BF16).astype(F32)
            middle = (level - high).astype(BF16).astype(F32)
            low = level - high - middle
            stats = jnp.concatenate([high, middle, low, jnp.zeros((4, TOK), F32)], axis=0)
            out_ref[HEADS * HD : HEADS * HD + 16, :] = stats.astype(BF16)


def attend(first, last, lengths, state, sources, bundles):
    operands = [lengths, *state, *bundles]
    running = [jax.ShapeDtypeStruct((1, ROWS), F32), jax.ShapeDtypeStruct((VROWS, ROWS), F32)]
    scratch = []
    if last:
        outs = [jax.ShapeDtypeStruct((HEADS * HD + 16, TOK), BF16)] * 4
        scratch = [pltpu.VMEM(r.shape, r.dtype) for r in running]
    elif first:
        outs = [
            jax.ShapeDtypeStruct((2 * HD, ROWS), BF16),
            jax.ShapeDtypeStruct((1, HEAD_ROWS), F32),
        ] + running
    else:
        outs = running
    if not last:
        held = 0 if first else state[-1].shape[0]
        outs = outs + [jax.ShapeDtypeStruct((held + len(sources) * 4 * FRESH, HD), BF16)]
    slots = len(sources) * SLOTS
    scratch += [
        pltpu.VMEM((slots, 2 * HD), BF16),
        pltpu.VMEM((VROWS, slots), BF16),
        pltpu.SMEM((slots // BLOCK + 1,), jnp.int32),
        pltpu.VMEM((2, BLOCK, HEAD_ROWS), F32),
        pltpu.VMEM((2, 1, HEAD_ROWS), F32),
    ]
    return pl.pallas_call(
        lambda *refs: attend_body(first, last, sources, *refs),
        out_shape=outs,
        in_specs=[SMEM] + [VMEM] * (len(operands) - 1),
        out_specs=[VMEM] * len(outs),
        scratch_shapes=scratch,
        compiler_params=params(26),
        cost_estimate=pl.CostEstimate(
            flops=10**6, bytes_accessed=2**10, transcendentals=0
        ),
        name="attend",
    )(*operands)


def merge_body(*refs):
    parts, out_ref = refs[:-1], refs[-1]
    levels = []
    for part in parts:
        coded = part[HEADS * HD : HEADS * HD + 16, :].astype(F32)
        levels.append(coded[0:4] + coded[4:8] + coded[8:12])
    top = levels[0]
    for level in levels[1:]:
        top = jnp.maximum(top, level)
    weights = [jnp.exp2(level - top) for level in levels]
    total = weights[0] + weights[1] + weights[2] + weights[3]
    weights = [w / total for w in weights]
    for head in range(HEADS):
        mixed = None
        for part, w in zip(parts, weights):
            term = part[head * HD : (head + 1) * HD, :].astype(F32) * w[head : head + 1]
            mixed = term if mixed is None else mixed + term
        out_ref[:, head * HD : (head + 1) * HD] = mixed.T.astype(BF16)


def merge(parts):
    return pl.pallas_call(
        merge_body,
        out_shape=jax.ShapeDtypeStruct((TOK, HEADS * HD), BF16),
        in_specs=[VMEM] * 4,
        out_specs=VMEM,
        compiler_params=params(4),
        name="merge",
    )(*parts)


def project_body(*refs):
    x_own, x_other = refs[0:2]
    weights = refs[2:4]
    out = refs[4:13]
    x_ref, w_ref, sems = refs[13:16]
    depth = weights[0].shape[0]
    copies = [
        pltpu.make_async_copy(weight, w_ref.at[pl.ds(i * depth, depth)], sems.at[i])
        for i, weight in enumerate(weights)
    ]
    for copy in copies:
        copy.start()
    z = lax.axis_index("z")
    for r in range(8):
        part = pl.multiple_of(lax.rem(z + r, 8) * 16, 16)
        for j in range(4):
            row = r * 64 + j * 16
            source = pl.ds(pl.multiple_of(part + j * TOK, 16), 16)
            x_ref[row : row + 16, 0:depth] = x_own[source, :]
            x_ref[row : row + 16, depth : 2 * depth] = x_other[source, :]
    for copy in copies:
        copy.wait()
    for n in range(4):
        cols = slice(n * 256, (n + 1) * 256)
        y = jnp.dot(x_ref[...], w_ref[:, cols], preferred_element_type=F32).astype(BF16)
        for r in range(8):
            if r < 4:
                out[r][:, cols] = y[r * 64 : (r + 1) * 64]
            elif r == 4:
                out[4][:, cols] = y[256:288]
                out[5][:, cols] = y[288:320]
            else:
                out[r + 1][:, cols] = y[r * 64 : (r + 1) * 64]


def project(x_own, x_other, weights):
    full = jax.ShapeDtypeStruct((64, WIDE), BF16)
    half = jax.ShapeDtypeStruct((32, WIDE), BF16)
    return pl.pallas_call(
        project_body,
        out_shape=[full] * 4 + [half] * 2 + [full] * 3,
        in_specs=[VMEM] * 2 + [HBM] * 2,
        out_specs=[VMEM] * 9,
        scratch_shapes=[
            pltpu.VMEM((512, 1024), BF16),
            pltpu.VMEM((1024, WIDE), BF16),
            pltpu.SemaphoreType.DMA((2,)),
        ],
        compiler_params=params(12),
        name="project",
    )(x_own, x_other, *weights)


def sum_bf16(a, b):
    return (a.astype(F32) + b.astype(F32)).astype(BF16)


def sum_over_z(parts):
    up = along_z(parts[4], 1)
    down = along_z(parts[5], -1)
    p3 = parts[3]
    half = p3.shape[0] // 2
    up = jnp.concatenate([sum_bf16(p3[:half], up), p3[half:]], axis=0)
    p5 = parts[6]
    down = jnp.concatenate([p5[:half], sum_bf16(p5[half:], down)], axis=0)
    for r in (2, 1):
        up = sum_bf16(parts[r], along_z(up, 1))
        down = sum_bf16(parts[9 - r], along_z(down, -1))
    return parts[0], along_z(up, 1), along_z(down, -1)


def order_body(*refs):
    out_ref = refs[6]
    yp, yl, xh = (lax.axis_index(name) for name in ("yp", "yl", "xh"))
    for side in range(2):
        kept, up, down = refs[side * 3 : side * 3 + 3]
        total = kept[...].astype(F32) + up[...].astype(F32) + down[...].astype(F32)
        total = total.astype(BF16)
        column = pl.ds(pl.multiple_of((yl if side == 0 else 1 - yl) * WIDE, WIDE), WIDE)
        for j in range(4):
            place = (yp if j % 2 == 0 else 1 - yp) * 2 + (xh if j < 2 else 1 - xh)
            out_ref[place, :, column] = total[j * 16 : (j + 1) * 16]


def ordered(sums):
    return pl.pallas_call(
        order_body,
        out_shape=jax.ShapeDtypeStruct((4, 16, 2 * WIDE), BF16),
        in_specs=[VMEM] * 6,
        out_specs=VMEM,
        compiler_params=params(4),
        name="ordered",
    )(*sums)


def finish_body(spread_ref, out_ref, sum_ref):
    yl = lax.axis_index("yl")
    for side in range(2):
        cols = slice(side * WIDE, (side + 1) * WIDE)
        for p in range(2):
            for xh in range(2):
                for core in range(2):
                    first = (p * 2 + xh) * 16 + core * 4
                    sum_ref[p, xh, core] = (
                        spread_ref[first : first + 4, cols].astype(F32)
                        + spread_ref[first + 8 : first + 12, cols].astype(F32)
                    )
        own = yl == side
        for p in range(2):
            for xh in range(2):
                for core in range(2):
                    value = sum_ref[p, xh, core]
                    if core == 1:
                        value = jnp.where(own, value, sum_ref[1 - p, xh, core])
                    start = (((p * 2 + side) * 2 + xh) * 2 + core) * WIDE
                    out_ref[:, start : start + WIDE] = value.astype(BF16)


def finish(spread):
    return pl.pallas_call(
        finish_body,
        out_shape=jax.ShapeDtypeStruct((4, 16 * WIDE), BF16),
        in_specs=[VMEM],
        out_specs=VMEM,
        scratch_shapes=[pltpu.VMEM((2, 2, 2, 4, WIDE), F32)],
        compiler_params=params(4),
        name="finish",
    )(spread)


def shards(
    queries, cache_keys, cache_values, new_keys, new_values, out_weight, cache_lengths, positions
):
    q_ext, kv = pack(
        queries, cache_keys[0, 0], cache_values[0, 0], new_keys, new_values, positions[None, :]
    )
    left, right = along_x(kv, 1), along_x(kv, -1)
    q_prev, q_next, q_far = along_y(q_ext, 1), along_y(q_ext, -1), along_y(q_ext, 2)
    q_all = (q_prev, q_next, q_far)
    w_kept, w_away = halves(after(out_weight, q_prev))
    other = to_other_core(after(kv, q_all))
    w_kept_pair, w_other_pair = to_y_pair(w_kept, False), to_y_pair(w_away, True)
    left, right = after((left, right), w_kept)
    far = along_x(after(kv, (left, right)), 2)
    rows_t, row_pos, m, acc, carry = attend(
        True,
        False,
        cache_lengths,
        (q_ext, *q_all),
        ((0, 0), (0, 1), (3, 0), (1, 0)),
        (kv, other, left, right),
    )
    left_other, right_other = to_other_core(left), to_other_core(right)
    far_other = to_other_core(after(far, m))
    mine, prev, following, distant = attend(
        False,
        True,
        cache_lengths,
        (rows_t, row_pos, m, acc, carry),
        ((3, 1), (1, 1), (2, 0), (2, 1)),
        (left_other, right_other, far, far_other),
    )
    attended = merge((mine, along_y(prev, -1), along_y(following, 1), along_y(distant, 2)))

    attended, w_kept_pair, w_other_pair = lax.optimization_barrier(
        (attended, w_kept_pair, w_other_pair)
    )
    w_other = to_other_core(w_away)

    corner = lax.ppermute(attended, ("yp", "xh"), [(i, 3 - i) for i in range(4)])
    blocks = (attended, along_y(attended, 2), along_x(attended, 2), corner)
    x_own = jnp.concatenate(blocks, axis=0)
    x_other = to_other_core(x_own)
    near = project(x_own, x_other, (w_kept, w_other))
    pair = project(x_own, x_other, (w_kept_pair, w_other_pair))
    blocks = ordered((*sum_over_z(near), *sum_over_z(pair))).reshape(64, 2 * WIDE)
    spread = lax.all_to_all(blocks, ("yp", "xh", "xl", "core"), 0, 0, tiled=True)
    return finish(spread)


def solution(mesh):
    fine = Mesh(
        mesh.devices.reshape(2, 2, 2, 8, 2, 2), ("yp", "yl", "xh", "z", "xl", "core")
    )
    seq, head = ("yp", "yl", "xh"), ("z", "xl", "core")
    placed = (
        P(seq, head),
        P(seq, head, None, None),
        P(seq, head, None, None),
        P(seq, None),
        P(seq, None),
        P(head, seq),
        P(),
        P(seq),
    )
    return jax.shard_map(
        shards, mesh=fine, in_specs=placed, out_specs=P(seq + head, None), check_vma=False
    )
```

```python
import math

import jax
import jax.numpy as jnp
from jax import lax
from jax.experimental import pallas as pl
from jax.experimental.pallas import tpu as pltpu
from jax.sharding import Mesh, PartitionSpec as P

HD = 128
HEADS = 4
TOK = 128
SLOTS = 1024
ROWS = 2048
HEAD_ROWS = 512
BLOCK = 1024
VROWS = HD + 16
NEG = -1e30
FRESH = 32
WIDE = 1024
TO_LOG2 = math.log2(math.e) / math.sqrt(HD)
F32 = jnp.float32
BF16 = jnp.bfloat16
VMEM = pl.BlockSpec(memory_space=pltpu.VMEM)
SMEM = pl.BlockSpec(memory_space=pltpu.SMEM)
HBM = pl.BlockSpec(memory_space=pltpu.HBM)


def moved(value, axis, size, step):
    return lax.ppermute(value, axis, [(i, (i + step) % size) for i in range(size)])


def along_y(value, step):
    return moved(value, ("yp", "yl"), 4, step)


def to_y_pair(value, swap):
    pairs = []
    for y in range(4):
        for core in range(2):
            there = 1 - core if swap else core
            other = y ^ 1 if there == 0 else (y + (1 if y % 2 else 3)) % 4
            pairs.append((y * 2 + core, other * 2 + there))
    return lax.ppermute(value, ("yp", "yl", "core"), pairs)


def y_index():
    return lax.axis_index("yp") * 2 + lax.axis_index("yl")


def along_x(value, step):
    return moved(value, ("xh", "xl"), 4, step)


def along_z(value, step):
    return moved(value, "z", 8, step)


def to_other_core(value):
    return moved(value, "core", 2, 1)


def after(value, earlier):
    return lax.optimization_barrier((value, earlier))[0]


def params(mib):
    return pltpu.CompilerParams(vmem_limit_bytes=mib * 2**20)


def pack_body(q_hbm, k_hbm, v_hbm, nk_hbm, nv_hbm, pos_ref, q_out, kv_out, col_ref, sems):
    z = lax.axis_index("z")
    quarter = lax.axis_index("xl") * 2 + lax.axis_index("core")
    lanes = pl.ds(pl.multiple_of(z * HD, HD), HD)
    rows = pl.ds(pl.multiple_of(quarter * FRESH, FRESH), FRESH)
    start = 2 * SLOTS
    copies = [
        pltpu.make_async_copy(source, target, sems.at[i])
        for i, (source, target) in enumerate(
            (
                (q_hbm, q_out.at[pl.ds(0, TOK)]),
                (k_hbm, kv_out.at[pl.ds(0, SLOTS)]),
                (v_hbm, kv_out.at[pl.ds(SLOTS, SLOTS)]),
                (nk_hbm.at[rows, lanes], kv_out.at[pl.ds(start, FRESH)]),
                (nv_hbm.at[rows, lanes], kv_out.at[pl.ds(start + FRESH, FRESH)]),
            )
        )
    ]
    for copy in copies:
        copy.start()
    pos = jnp.broadcast_to(pos_ref[...].astype(F32), (TOK, TOK))
    high = jnp.floor(pos * (1.0 / 128.0))
    low = pos - high * 128.0
    q_out[TOK : TOK + 16, :] = jnp.zeros((16, HEADS * HD), BF16)
    row = lax.broadcasted_iota(jnp.int32, (16, TOK), 0)
    coded = jnp.where(row == 0, high[0:16], jnp.where(row == 1, low[0:16], 0.0))
    q_out[TOK : TOK + 16, 0:TOK] = coded.astype(BF16)
    col_ref[...] = high.T
    kv_out[start + 2 * FRESH : start + 3 * FRESH, :] = col_ref[rows, :].astype(BF16)
    col_ref[...] = low.T
    kv_out[start + 3 * FRESH : start + 4 * FRESH, :] = col_ref[rows, :].astype(BF16)
    for copy in copies:
        copy.wait()


def pack(queries, keys, values, new_keys, new_values, positions):
    return pl.pallas_call(
        pack_body,
        out_shape=[
            jax.ShapeDtypeStruct((TOK + 16, HEADS * HD), BF16),
            jax.ShapeDtypeStruct((2 * SLOTS + 4 * FRESH, HD), BF16),
        ],
        in_specs=[HBM] * 5 + [VMEM],
        out_specs=[VMEM] * 2,
        scratch_shapes=[pltpu.VMEM((TOK, TOK), F32), pltpu.SemaphoreType.DMA((5,))],
        name="pack",
    )(queries, keys, values, new_keys, new_values, positions)


def halves_body(w_hbm, w_kept, w_away, sems):
    core = lax.axis_index("core")
    copies = [
        pltpu.make_async_copy(
            w_hbm.at[:, pl.ds(pl.multiple_of(half * WIDE, WIDE), WIDE)], target, sems.at[i]
        )
        for i, (half, target) in enumerate(((core, w_kept), (1 - core, w_away)))
    ]
    for copy in copies:
        copy.start()
    for copy in copies:
        copy.wait()


def halves(weight):
    return pl.pallas_call(
        halves_body,
        out_shape=[jax.ShapeDtypeStruct((weight.shape[0], WIDE), BF16)] * 2,
        in_specs=[HBM],
        out_specs=[VMEM] * 2,
        scratch_shapes=[pltpu.SemaphoreType.DMA((2,))],
        name="halves",
    )(weight)


def update(s, top, values_t, cols, m_ref, acc_ref):
    old = m_ref[:, cols]
    new = jnp.maximum(old, top)
    p = jnp.exp2(s - new).astype(BF16)
    m_ref[:, cols] = new
    acc_ref[:, cols] = acc_ref[:, cols] * jnp.exp2(old - new) + jnp.dot(
        values_t, p, preferred_element_type=F32
    )


def flash(block_count, base_ref, keys2, values_t, rows_t, m_ref, acc_ref, s_ref, top_ref):
    def place(step):
        cols = pl.multiple_of((step % HEADS) * HEAD_ROWS, HEAD_ROWS)
        base = pl.multiple_of(base_ref[step // HEADS], BLOCK)
        return pl.ds(base, BLOCK), pl.ds(cols, HEAD_ROWS)

    def score(step, slot):
        at, cols = place(step)
        s = jnp.dot(keys2[at, :], rows_t[:, cols], preferred_element_type=F32)
        s_ref[slot] = s
        top_ref[slot] = jnp.max(s, axis=0, keepdims=True)

    def settle(step, slot):
        at, cols = place(step)
        update(s_ref[slot], top_ref[slot], values_t[:, at], cols, m_ref, acc_ref)

    steps = block_count * HEADS

    @pl.when(steps > 0)
    def _():
        score(0, 0)

    @pl.loop(0, steps // 2)
    def _(i):
        score(2 * i + 1, 1)
        settle(2 * i, 0)
        score(jnp.minimum(2 * i + 2, steps - 1), 0)
        settle(2 * i + 1, 1)


def absorb_fresh(carry_ref, kv_refs, rows_t, row_pos, m_ref, acc_ref):
    def fresh(part):
        pieces = []
        for j in range(carry_ref.shape[0] // (4 * FRESH)):
            start = (j * 4 + part) * FRESH
            pieces.append(carry_ref[start : start + FRESH, :])
        for kv in kv_refs:
            start = 2 * SLOTS + part * FRESH
            pieces.append(kv[start : start + FRESH, :])
        return jnp.concatenate(pieces, axis=0)

    keys = fresh(0)
    keys = jnp.concatenate([keys, keys], axis=1)
    values = fresh(1).astype(F32).T
    ones = jnp.ones((VROWS - HD, values.shape[1]), F32)
    values_t = jnp.concatenate([values, ones], axis=0).astype(BF16)
    key_pos = fresh(2).astype(F32) * 128.0 + fresh(3).astype(F32)
    seen = jnp.concatenate([key_pos] * (HEAD_ROWS // TOK), axis=1) <= row_pos[...]

    def score(head):
        cols = slice(head * HEAD_ROWS, (head + 1) * HEAD_ROWS)
        s = jnp.dot(keys, rows_t[:, cols], preferred_element_type=F32)
        return jnp.where(seen, s, NEG)

    s = score(0)
    for head in range(HEADS):
        following = score(head + 1) if head + 1 < HEADS else None
        cols = slice(head * HEAD_ROWS, (head + 1) * HEAD_ROWS)
        top = jnp.max(s, axis=0, keepdims=True)
        update(s, top, values_t, cols, m_ref, acc_ref)
        s = following


def attend_body(first, last, sources, *refs):
    refs = list(refs)
    chunks = len(sources)
    len_ref = refs.pop(0)
    if first:
        q_refs = [refs.pop(0) for _ in range(4)]
    else:
        rows_t, row_pos, m_in, acc_in, carry_in = [refs.pop(0) for _ in range(5)]
    kv_refs = [refs.pop(0) for _ in range(chunks)]
    if last:
        out_refs = [refs.pop(0) for _ in range(4)]
    else:
        if first:
            rows_t, row_pos = refs.pop(0), refs.pop(0)
        m_out, acc_out, carry_out = [refs.pop(0) for _ in range(3)]
    if last:
        m_ref, acc_ref = refs.pop(0), refs.pop(0)
    else:
        m_ref, acc_ref = m_out, acc_out
    keys2, values_t, base_ref, s_ref, top_ref = refs

    if first:
        for i, q_ref in enumerate(q_refs):
            for head in range(HEADS):
                q = q_ref[0:TOK, head * HD : (head + 1) * HD].astype(F32).T * TO_LOG2
                high = q.astype(BF16)
                cols = slice(head * HEAD_ROWS + i * TOK, head * HEAD_ROWS + (i + 1) * TOK)
                rows_t[0:HD, cols] = high
                rows_t[HD : 2 * HD, cols] = (q - high.astype(F32)).astype(BF16)
            coded = q_ref[TOK : TOK + 16, 0:TOK].astype(F32)
            row_pos[:, i * TOK : (i + 1) * TOK] = coded[0:1] * 128.0 + coded[1:2]
        m_ref[...] = jnp.full(m_ref.shape, NEG, F32)
        acc_ref[...] = jnp.zeros(acc_ref.shape, F32)
    else:
        m_ref[...] = m_in[...]
        acc_ref[...] = acc_in[...]

    x = lax.axis_index("xh") * 2 + lax.axis_index("xl")
    block_count = jnp.int32(0)
    for j, (step, swapped) in enumerate(sources):
        there = lax.rem(x + step, 4)
        group = y_index() * 2 + there // 2
        quarter = lax.rem(there, 2) * 2 + lax.rem(lax.axis_index("core") + swapped, 2)
        live = jnp.clip(len_ref[group] - quarter * SLOTS, 0, SLOTS)
        at = slice(j * SLOTS, (j + 1) * SLOTS)
        alive = lax.broadcasted_iota(jnp.int32, (SLOTS, HD), 0) < live
        k = kv_refs[j][0:SLOTS, :].astype(F32)
        k = jnp.where(alive, k, k[0:1, :]).astype(BF16)
        keys2[at, 0:HD] = k
        keys2[at, HD : 2 * HD] = k
        alive = lax.broadcasted_iota(jnp.int32, (VROWS, SLOTS), 1) < live
        v = jnp.concatenate(
            [kv_refs[j][SLOTS : 2 * SLOTS, :].astype(F32).T, jnp.ones((VROWS - HD, SLOTS), F32)],
            axis=0,
        )
        values_t[:, at] = jnp.where(alive, v, 0.0).astype(BF16)
        for b in range(SLOTS // BLOCK):
            base_ref[block_count] = j * SLOTS + b * BLOCK
            block_count += (live > b * BLOCK).astype(jnp.int32)

    if not last:
        held = 0 if first else carry_in.shape[0]
        if held:
            carry_out[0:held, :] = carry_in[...]
        for j, kv in enumerate(kv_refs):
            at = held + j * 4 * FRESH
            carry_out[at : at + 4 * FRESH, :] = kv[2 * SLOTS : 2 * SLOTS + 4 * FRESH, :]
    else:
        absorb_fresh(carry_in, kv_refs, rows_t, row_pos, m_ref, acc_ref)

    flash(block_count, base_ref, keys2, values_t, rows_t, m_ref, acc_ref, s_ref, top_ref)

    if last:
        for i, out_ref in enumerate(out_refs):
            levels = []
            for head in range(HEADS):
                start = head * HEAD_ROWS + i * TOK
                cols = slice(start, start + TOK)
                total = acc_ref[HD : HD + 1, cols]
                out_ref[head * HD : (head + 1) * HD, :] = (acc_ref[0:HD, cols] / total).astype(BF16)
                levels.append(m_ref[:, cols] + jnp.log2(total))
            level = jnp.concatenate(levels, axis=0)
            high = level.astype(BF16).astype(F32)
            middle = (level - high).astype(BF16).astype(F32)
            low = level - high - middle
            stats = jnp.concatenate([high, middle, low, jnp.zeros((4, TOK), F32)], axis=0)
            out_ref[HEADS * HD : HEADS * HD + 16, :] = stats.astype(BF16)


def attend(first, last, lengths, state, sources, bundles):
    operands = [lengths, *state, *bundles]
    running = [jax.ShapeDtypeStruct((1, ROWS), F32), jax.ShapeDtypeStruct((VROWS, ROWS), F32)]
    scratch = []
    if last:
        outs = [jax.ShapeDtypeStruct((HEADS * HD + 16, TOK), BF16)] * 4
        scratch = [pltpu.VMEM(r.shape, r.dtype) for r in running]
    elif first:
        outs = [
            jax.ShapeDtypeStruct((2 * HD, ROWS), BF16),
            jax.ShapeDtypeStruct((1, HEAD_ROWS), F32),
        ] + running
    else:
        outs = running
    if not last:
        held = 0 if first else state[-1].shape[0]
        outs = outs + [jax.ShapeDtypeStruct((held + len(sources) * 4 * FRESH, HD), BF16)]
    slots = len(sources) * SLOTS
    scratch += [
        pltpu.VMEM((slots, 2 * HD), BF16),
        pltpu.VMEM((VROWS, slots), BF16),
        pltpu.SMEM((slots // BLOCK + 1,), jnp.int32),
        pltpu.VMEM((2, BLOCK, HEAD_ROWS), F32),
        pltpu.VMEM((2, 1, HEAD_ROWS), F32),
    ]
    return pl.pallas_call(
        lambda *refs: attend_body(first, last, sources, *refs),
        out_shape=outs,
        in_specs=[SMEM] + [VMEM] * (len(operands) - 1),
        out_specs=[VMEM] * len(outs),
        scratch_shapes=scratch,
        compiler_params=params(26),
        cost_estimate=pl.CostEstimate(
            flops=10**6, bytes_accessed=2**10, transcendentals=0
        ),
        name="attend",
    )(*operands)


def merge_body(*refs):
    parts, out_ref = refs[:-1], refs[-1]
    levels = []
    for part in parts:
        coded = part[HEADS * HD : HEADS * HD + 16, :].astype(F32)
        levels.append(coded[0:4] + coded[4:8] + coded[8:12])
    top = levels[0]
    for level in levels[1:]:
        top = jnp.maximum(top, level)
    weights = [jnp.exp2(level - top) for level in levels]
    total = weights[0] + weights[1] + weights[2] + weights[3]
    weights = [w / total for w in weights]
    for head in range(HEADS):
        mixed = None
        for part, w in zip(parts, weights):
            term = part[head * HD : (head + 1) * HD, :].astype(F32) * w[head : head + 1]
            mixed = term if mixed is None else mixed + term
        out_ref[:, head * HD : (head + 1) * HD] = mixed.T.astype(BF16)


def merge(parts):
    return pl.pallas_call(
        merge_body,
        out_shape=jax.ShapeDtypeStruct((TOK, HEADS * HD), BF16),
        in_specs=[VMEM] * 4,
        out_specs=VMEM,
        compiler_params=params(4),
        name="merge",
    )(*parts)


def project_body(*refs):
    x_own, x_other = refs[0:2]
    weights = refs[2:6]
    out = refs[6:15]
    x_ref, w_ref, sems = refs[15:18]
    depth = weights[0].shape[0]
    copies = [
        pltpu.make_async_copy(
            weight, w_ref.at[i // 2, pl.ds((i % 2) * depth, depth)], sems.at[i]
        )
        for i, weight in enumerate(weights)
    ]
    for copy in copies:
        copy.start()
    z = lax.axis_index("z")
    for r in range(8):
        part = pl.multiple_of(lax.rem(z + r, 8) * 16, 16)
        for j in range(2):
            row = r * 32 + j * 16
            source = pl.ds(pl.multiple_of(part + j * TOK, 16), 16)
            x_ref[row : row + 16, 0:depth] = x_own[source, :]
            x_ref[row : row + 16, depth : 2 * depth] = x_other[source, :]
    for side in range(2):
        for copy in copies[side * 2 : side * 2 + 2]:
            copy.wait()
        for n in range(4):
            cols = slice(n * 256, (n + 1) * 256)
            y = jnp.dot(x_ref[...], w_ref[side, :, cols], preferred_element_type=F32).astype(BF16)
            cols = slice(side * WIDE + n * 256, side * WIDE + (n + 1) * 256)
            for r in range(8):
                if r < 4:
                    out[r][:, cols] = y[r * 32 : (r + 1) * 32]
                elif r == 4:
                    out[4][:, cols] = y[128:144]
                    out[5][:, cols] = y[144:160]
                else:
                    out[r + 1][:, cols] = y[r * 32 : (r + 1) * 32]


def project(x_own, x_other, weights):
    full = jax.ShapeDtypeStruct((32, 2 * WIDE), BF16)
    half = jax.ShapeDtypeStruct((16, 2 * WIDE), BF16)
    return pl.pallas_call(
        project_body,
        out_shape=[full] * 4 + [half] * 2 + [full] * 3,
        in_specs=[VMEM] * 2 + [HBM] * 4,
        out_specs=[VMEM] * 9,
        scratch_shapes=[
            pltpu.VMEM((256, 1024), BF16),
            pltpu.VMEM((2, 1024, WIDE), BF16),
            pltpu.SemaphoreType.DMA((4,)),
        ],
        compiler_params=params(12),
        name="project",
    )(x_own, x_other, *weights)


def sum_bf16(a, b):
    return (a.astype(F32) + b.astype(F32)).astype(BF16)


def sum_over_z(parts):
    up = along_z(parts[4], 1)
    down = along_z(parts[5], -1)
    p3 = parts[3]
    half = p3.shape[0] // 2
    up = jnp.concatenate([sum_bf16(p3[:half], up), p3[half:]], axis=0)
    p5 = parts[6]
    down = jnp.concatenate([p5[:half], sum_bf16(p5[half:], down)], axis=0)
    for r in (2, 1):
        up = sum_bf16(parts[r], along_z(up, 1))
        down = sum_bf16(parts[9 - r], along_z(down, -1))
    return parts[0], along_z(up, 1), along_z(down, -1)


def order_body(*refs):
    out_ref = refs[6]
    yp, yl, xh = (lax.axis_index(name) for name in ("yp", "yl", "xh"))
    for pair in range(2):
        kept, up, down = refs[pair * 3 : pair * 3 + 3]
        total = kept[...].astype(F32) + up[...].astype(F32) + down[...].astype(F32)
        total = total.astype(BF16)
        for side in range(2):
            column = pl.ds(pl.multiple_of((yl if side == 0 else 1 - yl) * WIDE, WIDE), WIDE)
            for j in range(2):
                place = (yp if j == 0 else 1 - yp) * 2 + (xh if pair == 0 else 1 - xh)
                out_ref[place, :, column] = total[
                    j * 16 : (j + 1) * 16, side * WIDE : (side + 1) * WIDE
                ]


def ordered(sums):
    return pl.pallas_call(
        order_body,
        out_shape=jax.ShapeDtypeStruct((4, 16, 2 * WIDE), BF16),
        in_specs=[VMEM] * 6,
        out_specs=VMEM,
        compiler_params=params(4),
        name="ordered",
    )(*sums)


def finish_body(spread_ref, out_ref, sum_ref):
    yl = lax.axis_index("yl")
    for side in range(2):
        cols = slice(side * WIDE, (side + 1) * WIDE)
        for p in range(2):
            for xh in range(2):
                for core in range(2):
                    first = (p * 2 + xh) * 16 + core * 4
                    sum_ref[p, xh, core] = (
                        spread_ref[first : first + 4, cols].astype(F32)
                        + spread_ref[first + 8 : first + 12, cols].astype(F32)
                    )
        own = yl == side
        for p in range(2):
            for xh in range(2):
                for core in range(2):
                    value = sum_ref[p, xh, core]
                    if core == 1:
                        value = jnp.where(own, value, sum_ref[1 - p, xh, core])
                    start = (((p * 2 + side) * 2 + xh) * 2 + core) * WIDE
                    out_ref[:, start : start + WIDE] = value.astype(BF16)


def finish(spread):
    return pl.pallas_call(
        finish_body,
        out_shape=jax.ShapeDtypeStruct((4, 16 * WIDE), BF16),
        in_specs=[VMEM],
        out_specs=VMEM,
        scratch_shapes=[pltpu.VMEM((2, 2, 2, 4, WIDE), F32)],
        compiler_params=params(4),
        name="finish",
    )(spread)


def shards(
    queries, cache_keys, cache_values, new_keys, new_values, out_weight, cache_lengths, positions
):
    q_ext, kv = pack(
        queries, cache_keys[0, 0], cache_values[0, 0], new_keys, new_values, positions[None, :]
    )
    left, right = along_x(kv, 1), along_x(kv, -1)
    q_prev, q_next, q_far = along_y(q_ext, 1), along_y(q_ext, -1), along_y(q_ext, 2)
    q_all = (q_prev, q_next, q_far)
    w_kept, w_away = halves(after(out_weight, q_prev))
    other = to_other_core(after(kv, q_all))
    w_kept_pair, w_other_pair = to_y_pair(w_kept, False), to_y_pair(w_away, True)
    left, right = after((left, right), w_kept)
    far = along_x(after(kv, (left, right)), 2)
    rows_t, row_pos, m, acc, carry = attend(
        True,
        False,
        cache_lengths,
        (q_ext, *q_all),
        ((0, 0), (0, 1), (3, 0), (1, 0)),
        (kv, other, left, right),
    )
    left_other, right_other = to_other_core(left), to_other_core(right)
    far_other = to_other_core(after(far, m))
    mine, prev, following, distant = attend(
        False,
        True,
        cache_lengths,
        (rows_t, row_pos, m, acc, carry),
        ((3, 1), (1, 1), (2, 0), (2, 1)),
        (left_other, right_other, far, far_other),
    )
    attended = merge((mine, along_y(prev, -1), along_y(following, 1), along_y(distant, 2)))

    attended, w_kept_pair, w_other_pair = lax.optimization_barrier(
        (attended, w_kept_pair, w_other_pair)
    )

    w_other = to_other_core(after(w_away, attended))
    weights = (w_kept, w_other, w_kept_pair, w_other_pair)
    below, beside = along_y(attended, 2), along_x(attended, 2)
    corner = lax.ppermute(attended, ("yp", "xh"), [(i, 3 - i) for i in range(4)])
    near = jnp.concatenate([attended, below], axis=0)
    pair = jnp.concatenate([beside, corner], axis=0)
    near = project(near, to_other_core(near), weights)
    pair = project(pair, to_other_core(pair), weights)
    blocks = ordered((*sum_over_z(near), *sum_over_z(pair))).reshape(64, 2 * WIDE)
    spread = lax.all_to_all(blocks, ("yp", "xh", "xl", "core"), 0, 0, tiled=True)
    return finish(spread)


def solution(mesh):
    fine = Mesh(
        mesh.devices.reshape(2, 2, 2, 8, 2, 2), ("yp", "yl", "xh", "z", "xl", "core")
    )
    seq, head = ("yp", "yl", "xh"), ("z", "xl", "core")
    placed = (
        P(seq, head),
        P(seq, head, None, None),
        P(seq, head, None, None),
        P(seq, None),
        P(seq, None),
        P(head, seq),
        P(),
        P(seq),
    )
    return jax.shard_map(
        shards, mesh=fine, in_specs=placed, out_specs=P(seq + head, None), check_vma=False
    )
```
